256 devices in a mesh: row: 8 (over x, y_lo), col: 16 (over z, core), ch: 2 (over y_hi).
Axes of the slice: x: 4, y: 4 (y_hi: 2, y_lo: 2; y = y_hi * 2 + y_lo), z: 8, core: 2. Of those that a mesh axis runs over, the one named last changes fastest.
Arguments:
- tokens: bfloat16 [64, 256, 512], P('row', 'col'), may hold values from -6 to 6
- grad_output: bfloat16 [64, 256, 512], P('row', 'col'), may hold values from -6 to 6
- attn_gain: float32 [512], replicated, may hold values from 0.25 to 1.75
- mlp_gain: float32 [512], replicated, may hold values from 0.25 to 1.75
- w_qkv: bfloat16 [512, 3, 512], P(None, None, 'ch'), may hold values from -0.25 to 0.25
- w_out: bfloat16 [512, 512], P('ch'), may hold values from -0.25 to 0.25
- w_up: bfloat16 [512, 2, 2048], P(None, None, 'ch'), may hold values from -0.25 to 0.25
- w_down: bfloat16 [2048, 512], P('ch'), may hold values from -0.125 to 0.125
- head_scale: float32 [8], P('ch'), may hold values from 3 to 120, as said below
Outputs:
- out: bfloat16 [64, 256, 512], P('row', 'col')
- grad_input: bfloat16 [64, 256, 512], P('row', 'col')
- grad_qkv: bfloat16 [512, 3, 512], P(('row', 'col'), None, 'ch')
- grad_out_t: bfloat16 [512, 512], P(('row', 'col'), 'ch')
- grad_up: bfloat16 [512, 2, 2048], P(('row', 'col'), None, 'ch')
- grad_down_t: bfloat16 [512, 2048], P(('row', 'col'), 'ch')
The draws below stay inside these ranges and needn't reach their ends.
Inputs may be any that keep to these rules, and one draw needn't show every extreme that they name: `head_scale`: positive per-head score scale.
All inputs are finite; a program needn't handle non-finite values.
Results may differ from the reference program's by a relative error of at most 0.03.
The reference program's roundings to bfloat16 on the way count: a program that leaves them out, or rounds other values in their place, can miss the bound.
Values may be sent and summed in bfloat16 or wider, within the bound.
A program may use at most 128 MiB of HBM per device.

```python
import jax
import jax.numpy as jnp
from jax import lax

D = 512
HEADS = 8
FF = 2048
RADIUS = 7
TR = 8
TC = 16
GRID_ROWS = 64
GRID_COLS = 256
N_ROW = 8
N_COL = 16


def draw_head_scale(key, part):
    key = jax.random.fold_in(key, 11)
    lowest = 3.0
    highest = 30.0
    fraction = jax.random.uniform(key, (HEADS,), jnp.float32)
    return jnp.exp(jnp.log(lowest) + fraction * (jnp.log(highest) - jnp.log(lowest)))


def spiked(array, own_key, source, target, shards_of, factor):
    def block_of(dim):
        return (jnp.arange(array.shape[dim]) // (array.shape[dim] // shards_of)).reshape((-1,) + (1,) * (array.ndim - 1 - dim))

    near = jax.random.permutation(own_key, shards_of)[block_of(target)]
    other_side = (block_of(target) + shards_of // 2) % shards_of
    return jnp.where((block_of(source) == near) | (block_of(source) == other_side), factor * array, array)


def level_of(own_key, dims, cuts, smallest, top_value):
    loudness = 1.0
    for axis_at, parts in cuts:
        heights = jax.random.uniform(jax.random.fold_in(jax.random.fold_in(own_key, 6), axis_at), (parts,), jnp.float32, smallest / len(cuts), top_value / len(cuts))
        loudness = loudness * jnp.repeat(jnp.exp(heights), dims[axis_at] // parts).reshape((-1,) + (1,) * (len(dims) - 1 - axis_at))
    return loudness


def centred(own_key, extent, scale, most, cuts=(), held_as=jnp.bfloat16):
    values = jax.random.normal(own_key, extent, jnp.float32) * scale
    if len(cuts) > 0:
        values = level_of(own_key, extent, cuts, -0.22, 0.18) * values
    return jnp.clip(values, min=-most, max=most).astype(held_as)


def gaussian_with(own_key, shape, scale, limit, shards, heavy, kind=jnp.bfloat16):
    values = scale * jax.random.normal(own_key, shape, jnp.float32)
    if shards:
        values = values * level_of(own_key, shape, shards, -0.22, 0.18)
    return jnp.clip(spiked(values, jax.random.fold_in(own_key, 3), *heavy), -limit, limit).astype(kind)


def setup_inputs(seed: int = 0) -> dict:
    seeds = jax.random.split(jax.random.key(seed), 10)
    return {
        "tokens": gaussian_with(seeds[0], (GRID_ROWS, GRID_COLS, D), 1.0, 6.0, ((0, 8), (1, 16)), (1, 2, 16, 2.0)),
        "grad_output": gaussian_with(seeds[1], (GRID_ROWS, GRID_COLS, D), 1.0, 6.0, ((0, 8), (1, 16)), (1, 2, 16, 2.0)),
        "attn_gain": jnp.clip(1.0 + 0.15 * jax.random.normal(seeds[2], (D,), jnp.float32), 0.25, 1.75),
        "mlp_gain": jnp.clip(1.0 + 0.15 * jax.random.normal(seeds[3], (D,), jnp.float32), 0.25, 1.75),
        "w_qkv": centred(seeds[4], (D, 3, D), D ** -0.5, 0.25, ((2, 2),)),
        "w_out": centred(seeds[5], (D, D), D ** -0.5, 0.25, ((0, 2),)),
        "w_up": centred(seeds[6], (D, 2, FF), D ** -0.5, 0.25, ((2, 2),)),
        "w_down": centred(seeds[7], (FF, D), FF ** -0.5, 0.125, ((0, 2),)),
        "head_scale": draw_head_scale(jax.random.fold_in(seeds[9], 71), 0),
    }


eps = 1e-06

def normalize(values, gain):
    scale = lax.rsqrt(lax.optimization_barrier(jnp.mean(values * values, axis=-1, keepdims=True)) + eps)
    return values * scale * gain.astype(jnp.float32)

def normalize_back(values, gain, upstream):
    scale = lax.rsqrt(lax.optimization_barrier(jnp.mean(values * values, axis=-1, keepdims=True)) + eps)
    normed = values * scale
    incoming = upstream * gain.astype(jnp.float32)
    return scale * (incoming - normed * lax.optimization_barrier(jnp.mean(incoming * normed, axis=-1, keepdims=True)))

def gelu_parts(gate):
    cdf = 0.5 * (1.0 + jax.scipy.special.erf(gate * 0.7071067811865476))
    density = jnp.exp(-0.5 * gate * gate) * 0.3989422804014327
    return (gate * cdf, cdf + gate * density)

def key_rows(window, rows):
    width = window.shape[0] - rows + 1
    return jnp.stack([window[offset:offset + rows] for offset in range(width)], axis=1)

def fold_rows(stacked, rows):
    width = stacked.shape[1]
    total = jnp.zeros((rows + width - 1,) + stacked.shape[2:], jnp.float32)
    for offset in range(width):
        total = total.at[offset:offset + rows].add(stacked[:, offset])
    return total

def allowed_mask(inside, rows, cols, radius):
    inside_rows = jnp.transpose(key_rows(inside, rows), (1, 2, 0))
    key_col = jnp.arange(cols + 2 * radius, dtype=jnp.int32)[:, None]
    query_col = jnp.arange(cols, dtype=jnp.int32)[None, :]
    band = (key_col - query_col >= 0) & (key_col - query_col <= 2 * radius)
    return inside_rows[:, :, :, None] & band[None, :, None, :]

def tile_weights(queries, key_window, allowed):
    scores = jnp.einsum('rchd,rjkhd->hjkrc', queries.astype(jnp.float32), key_window.astype(jnp.float32))
    scores = jnp.where(allowed, scores, -1e+30)
    highest = lax.optimization_barrier(jnp.max(scores, axis=(1, 2), keepdims=True))
    raised = jnp.where(allowed, jnp.exp(scores - highest), 0.0)
    return raised / lax.optimization_barrier(jnp.sum(raised, axis=(1, 2), keepdims=True))

def through_norm(raw, norm, incoming, factor):
    along = lax.optimization_barrier(jnp.sum(raw * incoming, axis=-1, keepdims=True))
    return factor * norm * (incoming - norm * norm * raw * along)

def contract_rows(left, right):
    return lax.dot_general(left, right, (((0,), (0,)), ((), ())), preferred_element_type=jnp.float32)

def contract_cols(left, right):
    return lax.dot_general(left, right, (((1,), (1,)), ((), ())), preferred_element_type=jnp.float32)

def reference(tokens, grad_output, attn_gain, mlp_gain, w_qkv, w_out, w_up, w_down, head_scale):
    height, breadth, width = tokens.shape
    head_dim = width // HEADS
    count = height * breadth
    hidden_size = w_down.shape[0]
    edge = 2 * RADIUS
    flat_in = tokens.reshape(count, width).astype(jnp.float32)
    flat_grad = grad_output.reshape(count, width)
    attn_in = normalize(flat_in, attn_gain).astype(jnp.bfloat16)
    projected = jnp.dot(attn_in, w_qkv.reshape(width, 3 * width), preferred_element_type=jnp.float32)
    projected = projected.reshape(count, 3, HEADS, head_dim)
    query_raw = projected[:, 0]
    key_raw = projected[:, 1]
    query_norm = lax.rsqrt(lax.optimization_barrier(jnp.sum(query_raw * query_raw, axis=-1, keepdims=True)) + eps)
    key_norm = lax.rsqrt(lax.optimization_barrier(jnp.sum(key_raw * key_raw, axis=-1, keepdims=True)) + eps)
    scale = head_scale.astype(jnp.float32)[:, None]
    queries = (query_raw * query_norm * scale).astype(jnp.bfloat16)
    keys = (key_raw * key_norm).astype(jnp.bfloat16)
    values = projected[:, 2].astype(jnp.bfloat16)
    query_grid = queries.reshape(height, breadth, HEADS, head_dim)
    padding = ((RADIUS, RADIUS), (RADIUS, RADIUS), (0, 0), (0, 0))
    key_pad = jnp.pad(keys.reshape(height, breadth, HEADS, head_dim), padding)
    value_pad = jnp.pad(values.reshape(height, breadth, HEADS, head_dim), padding)
    tiles = jnp.arange(N_ROW * N_COL, dtype=jnp.int32)
    zero = jnp.zeros((), jnp.int32)
    window_shape = (TR + edge, TC + edge, HEADS, head_dim)

    def corner(index):
        first_row = (index // N_COL * TR).astype(jnp.int32)
        first_col = (index % N_COL * TC).astype(jnp.int32)
        return (first_row, first_col)

    def gather_tile(index):
        first_row, first_col = corner(index)
        query_tile = lax.dynamic_slice(query_grid, (first_row, first_col, zero, zero), (TR, TC, HEADS, head_dim))
        key_tile = key_rows(lax.dynamic_slice(key_pad, (first_row, first_col, zero, zero), window_shape), TR)
        value_tile = key_rows(lax.dynamic_slice(value_pad, (first_row, first_col, zero, zero), window_shape), TR)
        row_ids = first_row - RADIUS + jnp.arange(TR + edge, dtype=jnp.int32)
        col_ids = first_col - RADIUS + jnp.arange(TC + edge, dtype=jnp.int32)
        inside = ((row_ids >= 0) & (row_ids < height))[:, None] & ((col_ids >= 0) & (col_ids < breadth))[None, :]
        return (query_tile, key_tile, value_tile, allowed_mask(inside, TR, TC, RADIUS))

    def forward_tile(index):
        query_tile, key_tile, value_tile, allowed = gather_tile(index)
        weights = tile_weights(query_tile, key_tile, allowed).astype(jnp.bfloat16)
        result = jnp.einsum('hjkrc,rjkhd->rchd', weights.astype(jnp.float32), value_tile.astype(jnp.float32))
        return result.astype(jnp.bfloat16)

    def untile(stacked):
        grid = stacked.reshape(N_ROW, N_COL, TR, TC, HEADS, head_dim)
        return jnp.transpose(grid, (0, 2, 1, 3, 4, 5)).reshape(count, HEADS, head_dim)
    attended = untile(lax.map(forward_tile, tiles)).reshape(count, width)
    residual = flat_in + jnp.dot(attended, w_out, preferred_element_type=jnp.float32)
    mlp_in = normalize(residual, mlp_gain).astype(jnp.bfloat16)
    mixed = jnp.dot(mlp_in, w_up.reshape(width, 2 * hidden_size), preferred_element_type=jnp.float32)
    mixed = mixed.reshape(count, 2, hidden_size)
    gate = mixed[:, 0]
    value_part = mixed[:, 1]
    activated, slope = gelu_parts(gate)
    hidden = (activated * value_part).astype(jnp.bfloat16)
    out = (residual + jnp.dot(hidden, w_down, preferred_element_type=jnp.float32)).astype(jnp.bfloat16)
    grad_hidden = contract_cols(flat_grad, w_down)
    grad_mix = jnp.stack([grad_hidden * value_part * slope, grad_hidden * activated], axis=1).astype(jnp.bfloat16)
    grad_mix = grad_mix.reshape(count, 2 * hidden_size)
    grad_mlp_in = contract_cols(grad_mix, w_up.reshape(width, 2 * hidden_size))
    grad_resid = flat_grad.astype(jnp.float32) + normalize_back(residual, mlp_gain, grad_mlp_in)
    grad_resid_low = grad_resid.astype(jnp.bfloat16)
    grad_attended = contract_cols(grad_resid_low, w_out).astype(jnp.bfloat16)
    grad_grid = grad_attended.reshape(height, breadth, HEADS, head_dim)

    def backward_tile(carry, index):
        key_acc, value_acc = carry
        first_row, first_col = corner(index)
        query_tile, key_tile, value_tile, allowed = gather_tile(index)
        grad_tile = lax.dynamic_slice(grad_grid, (first_row, first_col, zero, zero), (TR, TC, HEADS, head_dim))
        weights = tile_weights(query_tile, key_tile, allowed)
        weights_low = weights.astype(jnp.bfloat16).astype(jnp.float32)
        grad_weights = jnp.einsum('rchd,rjkhd->hjkrc', grad_tile.astype(jnp.float32), value_tile.astype(jnp.float32))
        delta = lax.optimization_barrier(jnp.sum(weights * grad_weights, axis=(1, 2), keepdims=True))
        grad_scores = (weights * (grad_weights - delta)).astype(jnp.bfloat16).astype(jnp.float32)
        grad_query = jnp.einsum('hjkrc,rjkhd->rchd', grad_scores, key_tile.astype(jnp.float32))
        grad_key = fold_rows(jnp.einsum('hjkrc,rchd->rjkhd', grad_scores, query_tile.astype(jnp.float32)), TR)
        grad_value = fold_rows(jnp.einsum('hjkrc,rchd->rjkhd', weights_low, grad_tile.astype(jnp.float32)), TR)
        start = (first_row, first_col, zero, zero)
        key_acc = lax.dynamic_update_slice(key_acc, lax.dynamic_slice(key_acc, start, window_shape) + grad_key, start)
        value_acc = lax.dynamic_update_slice(value_acc, lax.dynamic_slice(value_acc, start, window_shape) + grad_value, start)
        return ((key_acc, value_acc), grad_query)
    empty = jnp.zeros((height + edge, breadth + edge, HEADS, head_dim), jnp.float32)
    carried, grad_queries = lax.scan(backward_tile, (empty, empty), tiles)
    grad_query_hat = untile(grad_queries)
    grad_key_hat = carried[0][RADIUS:RADIUS + height, RADIUS:RADIUS + breadth].reshape(count, HEADS, head_dim)
    grad_value_all = carried[1][RADIUS:RADIUS + height, RADIUS:RADIUS + breadth].reshape(count, HEADS, head_dim)
    grad_query_raw = through_norm(query_raw, query_norm, grad_query_hat, scale)
    grad_key_raw = through_norm(key_raw, key_norm, grad_key_hat, 1.0)
    grad_proj = jnp.stack([grad_query_raw, grad_key_raw, grad_value_all], axis=1).astype(jnp.bfloat16)
    grad_proj = grad_proj.reshape(count, 3 * width)
    grad_attn_in = contract_cols(grad_proj, w_qkv.reshape(width, 3 * width))
    grad_input = (grad_resid + normalize_back(flat_in, attn_gain, grad_attn_in)).astype(jnp.bfloat16)
    grad_qkv = contract_rows(attn_in, grad_proj).astype(jnp.bfloat16).reshape(width, 3, width)
    grad_up = contract_rows(mlp_in, grad_mix).astype(jnp.bfloat16).reshape(width, 2, hidden_size)
    grad_out_t = contract_rows(grad_resid_low, attended).astype(jnp.bfloat16)
    grad_down_t = contract_rows(flat_grad, hidden).astype(jnp.bfloat16)
    return (out.reshape(height, breadth, width), grad_input.reshape(height, breadth, width), grad_qkv, grad_out_t, grad_up, grad_down_t)
```

```python
import jax
import jax.numpy as jnp
from jax import lax
from jax.experimental import pallas as pl
from jax.experimental.pallas import tpu as pltpu
from jax.sharding import PartitionSpec as P

HEADS = 8
RADIUS = 7
EPS = 1e-06
MESH = pl.DeviceIdType.MESH
F32 = jnp.float32
BF16 = jnp.bfloat16

TOK = 128
HALF = 64
KEYS = 768
WIDTH = 512
INNER = 256
HID = 1024
NROW, NCOL = 8, 16
NX, NZ = 4, 8


def nn(a, b):
    return lax.dot_general(a, b, (((1,), (0,)), ((), ())), preferred_element_type=F32)


def nt(a, b):
    return lax.dot_general(a, b, (((1,), (1,)), ((), ())), preferred_element_type=F32)


def tn(a, b):
    return lax.dot_general(a, b, (((0,), (0,)), ((), ())), preferred_element_type=F32)


def erf(x):
    return lax.erf(x)


def norm_scale(v):
    return lax.rsqrt(jnp.mean(v * v, axis=-1, keepdims=True) + EPS)


def norm_back(v, gain, upstream):
    s = norm_scale(v)
    n = v * s
    e = upstream * gain
    return s * (e - n * jnp.mean(e * n, axis=-1, keepdims=True))


def to_halves(block):
    return jnp.concatenate(
        [block[:, :8].reshape(HALF, WIDTH), block[:, 8:].reshape(HALF, WIDTH)], axis=0
    )


def from_halves(flat):
    return jnp.concatenate(
        [flat[:HALF].reshape(8, 8, WIDTH), flat[HALF:].reshape(8, 8, WIDTH)], axis=1
    )


class Links:
    def __init__(self, send, recv):
        self.send, self.recv, self.count, self.open = send, recv, 0, []

    def start(self, src, dst, device):
        copy = pltpu.make_async_remote_copy(
            src_ref=src,
            dst_ref=dst,
            send_sem=self.send.at[self.count],
            recv_sem=self.recv.at[self.count],
            device_id=device,
            device_id_type=MESH,
        )
        self.count += 1
        copy.start()
        self.open.append(copy)
        return copy

    def finish(self):
        for copy in self.open:
            copy.wait_send()


class Piece:
    def __init__(self, links, place, refs, out):
        self.links, self.place, self.out = links, place, out
        self.part, self.rc, self.xs, self.rx, self.ys, self.ry, self.zs, self.rz, self.fs = refs

    def core(self):
        core = self.place["core"]
        self.copy = self.links.start(
            self.part.at[1 - core], self.rc, self.place["core_peer"]
        )

    def x(self):
        p = self.place
        self.copy.wait_recv()
        for i in range(NX):
            rows = pl.ds(i * 128, 128)
            mine = self.part[p["core"], rows, :].astype(F32)
            self.xs[i] = (mine + self.rc[rows, :].astype(F32)).astype(BF16)
        self.copies = [
            self.links.start(
                self.xs.at[lax.rem(p["x"] + d, NX)], self.rx.at[d - 1], p["x_peer"][d]
            )
            for d in range(1, NX)
        ]

    def y(self):
        p = self.place
        for copy in self.copies:
            copy.wait_recv()
        total = self.xs[p["x"]].astype(F32)
        for d in range(NX - 1):
            total = total + self.rx[d].astype(F32)
        total = total.astype(BF16)
        self.ys[0] = total[:64]
        self.ys[1] = total[64:]
        self.copy = self.links.start(self.ys.at[1 - p["y"]], self.ry, p["y_peer"])

    def z(self):
        p = self.place
        self.copy.wait_recv()
        total = (self.ys[p["y"]].astype(F32) + self.ry[...].astype(F32)).astype(BF16)
        wide = total.shape[1] // 2
        for low in range(2):
            for high in range(4):
                self.zs[2 * high + low] = total[
                    16 * high : 16 * high + 16, low * wide : (low + 1) * wide
                ]
        self.copies = [
            self.links.start(
                self.zs.at[lax.rem(p["z"] + d, NZ)], self.rz.at[d - 1], p["z_peer"][d]
            )
            for d in range(1, NZ)
        ]

    def regather(self):
        p = self.place
        for copy in self.copies:
            copy.wait_recv()
        total = self.zs[p["z"]].astype(F32)
        for d in range(NZ - 1):
            total = total + self.rz[d].astype(F32)
        slot = 2 * p["core"] + p["z_low"]
        self.fs[slot] = total.astype(BF16)
        self.copies = [
            self.links.start(self.fs.at[slot], self.fs.at[slot], device)
            for device in p["near_peers"]
        ]

    def store(self):
        p = self.place
        for copy in self.copies:
            copy.wait_recv()
        for slot in range(4):
            rows = self.fs[slot].astype(F32)
            rows = jnp.where(p["z_low"] == 0, rows[:8], rows[8:])
            rows = jnp.where(p["core"] == 0, rows[:4], rows[4:])
            wide = rows.shape[1]
            self.out[:, slot * wide : (slot + 1) * wide] = rows.astype(BF16)


PIECES = (1024, 2048, 512, 512)


def piece_scratch(n):
    return [
        pltpu.VMEM((2, WIDTH, n // 2), BF16),
        pltpu.VMEM((WIDTH, n // 2), BF16),
        pltpu.VMEM((NX, 128, n // 2), BF16),
        pltpu.VMEM((NX - 1, 128, n // 2), BF16),
        pltpu.VMEM((2, 64, n // 2), BF16),
        pltpu.VMEM((64, n // 2), BF16),
        pltpu.VMEM((NZ, 16, n // 4), BF16),
        pltpu.VMEM((NZ - 1, 16, n // 4), BF16),
        pltpu.VMEM((4, 16, n // 4), BF16),
    ]


PER_PIECE = 9
MESSAGES = 96


def kernel(*refs):
    (tok, gout, attn_gain, mlp_gain, head_scale, wqkv_h, wout_h, wup_h, wdown_h) = refs[:9]
    (out_o, gin_o, gdown_o, gup_o, goq_o, gkv_o) = refs[9:15]
    refs = refs[15:]
    piece_refs = [refs[i * PER_PIECE : (i + 1) * PER_PIECE] for i in range(len(PIECES))]
    (
        wqkv,
        wout,
        wup,
        wdown,
        win,
        qmask,
        gmask,
        bias,
        probs,
        plow,
        dprob,
        dscore,
        raw,
        resid,
        gresid,
        ain,
        mlpin,
        fgrad,
        att,
        ghid,
        hidden,
        gmix,
        gproj,
        sums,
        sums_in,
        acc,
        rim_out,
        rim_in,
        ver_out,
        ver_in,
        send_sem,
        recv_sem,
        local_sem,
    ) = refs[len(PIECES) * PER_PIECE :]

    row, col, ch = lax.axis_index("row"), lax.axis_index("col"), lax.axis_index("ch")
    x, y = row // 2, lax.rem(row, 2)
    z, core = col // 2, lax.rem(col, 2)
    z_low = lax.rem(z, 2)
    above = (lax.rem(row + NROW - 1, NROW), col, ch)
    below = (lax.rem(row + 1, NROW), col, ch)
    left = (row, lax.rem(col + NCOL - 1, NCOL), ch)
    right = (row, lax.rem(col + 1, NCOL), ch)
    twin = (row, col, 1 - ch)
    z_flip = z + 1 - 2 * z_low
    x_peer = [(lax.rem(x + d, NX) * 2 + y, col, ch) for d in range(NX)]
    z_peer = [(row, lax.rem(z + d, NZ) * 2 + core, ch) for d in range(NZ)]
    core_peer = (row, z * 2 + 1 - core, ch)
    across = (row, z_flip * 2 + 1 - core, ch)
    place = {
        "x": x,
        "y": y,
        "z": z,
        "core": core,
        "z_low": z_low,
        "core_peer": core_peer,
        "y_peer": (x * 2 + 1 - y, col, ch),
        "x_peer": x_peer,
        "z_peer": z_peer,
        "near_peers": [core_peer, (row, z_flip * 2 + core, ch), across],
    }
    links = Links(send_sem, recv_sem)
    outs = (gdown_o, gup_o, goq_o, gkv_o)
    down_p, up_p, oq_p, kv_p = [
        Piece(links, place, r, o) for r, o in zip(piece_refs, outs)
    ]

    loads = []
    for i, (src, dst) in enumerate(
        ((wqkv_h, wqkv), (wdown_h, wdown), (wout_h, wout), (wup_h, wup))
    ):
        load = pltpu.make_async_copy(src, dst, local_sem.at[i])
        load.start()
        loads.append(load)

    barrier = pltpu.get_barrier_semaphore()
    peers = [above, below, left, right, twin, across] + x_peer[1:] + z_peer[1:]
    for peer in peers:
        pl.semaphore_signal(barrier, inc=1, device_id=peer, device_id_type=MESH)

    lane = lax.broadcasted_iota(jnp.int32, (1, INNER), 1) // 64
    same_head = (
        lax.broadcasted_iota(jnp.int32, (INNER, INNER), 0) // 64
        == lax.broadcasted_iota(jnp.int32, (INNER, INNER), 1) // 64
    )
    ones = jnp.where(same_head, 1.0, 0.0).astype(BF16)

    def head_sum(values):
        high = values.astype(BF16)
        low = (values - high.astype(F32)).astype(BF16)
        return nn(high, ones) + nn(low, ones)

    def head_rows(values):
        return [jnp.where(lane == h, values, jnp.zeros_like(values)) for h in range(4)]

    scale = jnp.zeros((1, INNER), F32)
    for h in range(4):
        scale = jnp.where(lane == h, head_scale[h], scale)

    toks = to_halves(tok[...].astype(F32))
    a = (toks * norm_scale(toks) * attn_gain[...]).astype(BF16)
    ain[...] = a
    fgrad[...] = to_halves(gout[...].astype(F32)).astype(BF16)
    loads[0].wait()
    key_raw = nn(a, wqkv[:, INNER : 2 * INNER])
    key_norm = lax.rsqrt(head_sum(key_raw * key_raw) + EPS)
    keys = (key_raw * key_norm).astype(BF16)
    win[0, 1, 1] = keys[:HALF]
    win[0, 2, 1] = keys[HALF:]
    raw[2] = key_raw
    raw[3] = key_norm
    pl.semaphore_wait(barrier, len(peers))

    def vertical(kv):
        return [
            links.start(win.at[kv, pl.ds(1, 2), 1], win.at[kv, pl.ds(1, 2), 0], below),
            links.start(win.at[kv, pl.ds(1, 2), 1], win.at[kv, pl.ds(1, 2), 2], above),
        ]

    def horizontal(kv, i):
        return [
            links.start(win.at[kv, 2, i], win.at[kv, 0, i], right),
            links.start(win.at[kv, 1, i], win.at[kv, 3, i], left),
        ]

    key_vert = vertical(0)
    key_side = horizontal(0, 1)
    values = nn(a, wqkv[:, 2 * INNER :]).astype(BF16)
    win[1, 1, 1] = values[:HALF]
    win[1, 2, 1] = values[HALF:]
    value_vert = vertical(1)
    value_side = horizontal(1, 1)

    query_raw = nn(a, wqkv[:, :INNER])
    query_norm = lax.rsqrt(head_sum(query_raw * query_raw) + EPS)
    raw[0] = query_raw
    raw[1] = query_norm
    queries = (query_raw * query_norm * scale).astype(BF16)
    for h, part in enumerate(head_rows(queries)):
        qmask[h * TOK : (h + 1) * TOK, :] = part

    def bias_rows(i, carry):
        t = lax.broadcasted_iota(jnp.int32, (32, KEYS), 0) + i * 32
        k = lax.broadcasted_iota(jnp.int32, (32, KEYS), 1)
        j = (
            jnp.where(k >= 192, 1, 0) + jnp.where(k >= 384, 1, 0) + jnp.where(k >= 576, 1, 0)
        )
        in_strip = k - 192 * j
        key_row = (in_strip >> 3) - 8
        key_col = (j - 1) * 8 + (k & 7)
        query_row = (t & 63) >> 3
        query_col = (t >> 6) * 8 + (t & 7)
        down, across_by = key_row - query_row, key_col - query_col
        at_row, at_col = row * 8 + key_row, col * 16 + key_col
        ok = (down >= -RADIUS) & (down <= RADIUS)
        ok = ok & (across_by >= -RADIUS) & (across_by <= RADIUS)
        ok = ok & (at_row >= 0) & (at_row < 8 * NROW) & (at_col >= 0) & (at_col < 16 * NCOL)
        bias[pl.ds(pl.multiple_of(i * 32, 32), 32), :] = jnp.where(ok, 0.0, -1e30)
        return carry

    lax.fori_loop(0, 4, bias_rows, 0)

    loads[1].wait()
    ghid[...] = nt(fgrad[...], wdown[...])

    for copy in key_vert:
        copy.wait_recv()
    key_side += horizontal(0, 0) + horizontal(0, 2)
    for copy in value_vert:
        copy.wait_recv()
    value_side += horizontal(1, 0) + horizontal(1, 2)
    for copy in key_side:
        copy.wait_recv()

    key_window = win[0].reshape(KEYS, INNER)
    probs[...] = nt(qmask[...], key_window)

    def softmax_rows(i, carry):
        rows = pl.ds(pl.multiple_of(i * 32, 32), 32)
        s = probs[rows, :] + bias[pl.ds(pl.multiple_of((i % 4) * 32, 32), 32), :]
        e = jnp.exp(s - jnp.max(s, axis=-1, keepdims=True))
        p = e * (1.0 / jnp.sum(e, axis=-1, keepdims=True))
        probs[rows, :] = p
        plow[rows, :] = p.astype(BF16)
        return carry

    lax.fori_loop(0, 16, softmax_rows, 0)
    for copy in value_side:
        copy.wait_recv()
    value_window = win[1].reshape(KEYS, INNER)

    def fold_heads(stacked):
        total = jnp.where(lane == 0, stacked[:TOK], 0.0)
        for h in range(1, 4):
            total = total + jnp.where(lane == h, stacked[h * TOK : (h + 1) * TOK], 0.0)
        return total

    attended = fold_heads(nn(plow[...], value_window)).astype(BF16)
    att[...] = attended
    loads[2].wait()

    def exchange(slot, value):
        sums[slot] = value.astype(BF16)
        return links.start(sums.at[slot], sums_in.at[slot], twin)

    def total_of(slot, copy):
        copy.wait_recv()
        return sums[slot].astype(F32) + sums_in[slot].astype(F32)

    attn_sum = exchange(0, nn(attended, wout[...]))
    loads[3].wait()
    residual = to_halves(tok[...].astype(F32)) + total_of(0, attn_sum)
    resid[...] = residual
    m = (residual * norm_scale(residual) * mlp_gain[...]).astype(BF16)
    mlpin[...] = m

    for j in range(4):
        cols = slice(j * 256, (j + 1) * 256)
        cols_v = slice(HID + j * 256, HID + (j + 1) * 256)
        gate = nn(m, wup[:, cols])
        val = nn(m, wup[:, cols_v])
        cdf = 0.5 * (1.0 + erf(gate * 0.7071067811865476))
        density = jnp.exp(-0.5 * gate * gate) * 0.3989422804014327
        act = gate * cdf
        hidden[:, cols] = (act * val).astype(BF16)
        gh = ghid[:, cols]
        gmix[:, cols] = (gh * val * (cdf + gate * density)).astype(BF16)
        gmix[:, cols_v] = (gh * act).astype(BF16)
    mlp_back = exchange(1, nt(gmix[...], wup[...]))
    mlp_sum = exchange(2, nn(hidden[...], wdown[...]))

    down_p.part[0] = tn(fgrad[...], hidden[:, :512]).astype(BF16)
    down_p.part[1] = tn(fgrad[...], hidden[:, 512:]).astype(BF16)
    down_p.core()
    up_p.part[0] = tn(mlpin[...], gmix[:, :HID]).astype(BF16)
    up_p.part[1] = tn(mlpin[...], gmix[:, HID:]).astype(BF16)
    up_p.core()
    down_p.x()

    grad_resid = to_halves(gout[...].astype(F32)) + norm_back(
        resid[...], mlp_gain[...], total_of(1, mlp_back)
    )
    gresid[...] = grad_resid
    grad_low = grad_resid.astype(BF16)
    grad_att = nt(grad_low, wout[...]).astype(BF16)
    for h, part in enumerate(head_rows(grad_att)):
        gmask[h * TOK : (h + 1) * TOK, :] = part

    def rims(kv, whole):
        whole = whole.reshape(4, 3, HALF, INNER)
        acc[kv] = whole[1:3]
        rim_out[kv, 0] = whole[0].astype(BF16)
        rim_out[kv, 1] = whole[3].astype(BF16)
        return [
            links.start(rim_out.at[kv, 0], rim_in.at[kv, 0], left),
            links.start(rim_out.at[kv, 1], rim_in.at[kv, 1], right),
        ]

    value_rims = rims(1, tn(plow[...], gmask[...]))
    dprob[...] = nt(gmask[...], win[1].reshape(KEYS, INNER))

    def score_rows(i, carry):
        rows = pl.ds(pl.multiple_of(i * 32, 32), 32)
        p, g = probs[rows, :], dprob[rows, :]
        delta = jnp.sum(p * g, axis=-1, keepdims=True)
        dscore[rows, :] = (p * (g - delta)).astype(BF16)
        return carry

    lax.fori_loop(0, 16, score_rows, 0)
    key_rims = rims(0, tn(dscore[...], qmask[...]))

    def through_norm(which, incoming, factor):
        v, r = raw[2 * which], raw[2 * which + 1]
        along = head_sum(v * incoming)
        return factor * r * (incoming - r * r * v * along)

    grad_query = fold_heads(nn(dscore[...], win[0].reshape(KEYS, INNER)))
    gproj[:, :INNER] = through_norm(0, grad_query, scale).astype(BF16)
    oq_p.part[0] = tn(gresid[...].astype(BF16), att[...]).astype(BF16)
    oq_p.part[1] = tn(ain[...], gproj[:, :INNER]).astype(BF16)
    oq_p.core()

    def turn(kv, copies):
        for copy in copies:
            copy.wait_recv()
        acc[kv, 1] = acc[kv, 1] + rim_in[kv, 0].astype(F32)
        acc[kv, 0] = acc[kv, 0] + rim_in[kv, 1].astype(F32)
        ver_out[kv, 0] = acc[kv, :, 0].astype(BF16)
        ver_out[kv, 1] = acc[kv, :, 2].astype(BF16)
        return [
            links.start(ver_out.at[kv, 0], ver_in.at[kv, 0], above),
            links.start(ver_out.at[kv, 1], ver_in.at[kv, 1], below),
        ]

    value_turn = turn(1, value_rims)
    key_turn = turn(0, key_rims)
    up_p.x()
    out_o[...] = from_halves(resid[...] + total_of(2, mlp_sum)).astype(BF16)
    oq_p.x()
    down_p.y()

    def owned(kv, copies):
        for copy in copies:
            copy.wait_recv()
        mine = acc[kv, :, 1] + ver_in[kv, 0].astype(F32) + ver_in[kv, 1].astype(F32)
        return mine.reshape(TOK, INNER)

    gproj[:, 2 * INNER :] = owned(1, value_turn).astype(BF16)
    gproj[:, INNER : 2 * INNER] = through_norm(1, owned(0, key_turn), 1.0).astype(BF16)
    in_back = exchange(3, nt(gproj[...], wqkv[...]))
    kv_p.part[0] = tn(ain[...], gproj[:, INNER : 2 * INNER]).astype(BF16)
    kv_p.part[1] = tn(ain[...], gproj[:, 2 * INNER :]).astype(BF16)
    kv_p.core()
    up_p.y()
    oq_p.y()
    down_p.z()
    kv_p.x()
    grad_in = gresid[...] + norm_back(
        to_halves(tok[...].astype(F32)), attn_gain[...], total_of(3, in_back)
    )
    gin_o[...] = from_halves(grad_in).astype(BF16)
    up_p.z()
    oq_p.z()
    kv_p.y()
    down_p.regather()
    up_p.regather()
    kv_p.z()
    oq_p.regather()
    kv_p.regather()
    down_p.store()
    up_p.store()
    oq_p.store()
    kv_p.store()
    links.finish()


def shards(tokens, grad_output, attn_gain, mlp_gain, w_qkv, w_out, w_up, w_down, head_scale):
    rows, cols, width = tokens.shape
    vmem = pl.BlockSpec(memory_space=pltpu.VMEM)
    anywhere = pl.BlockSpec(memory_space=pl.ANY)
    out_shape = [
        jax.ShapeDtypeStruct(tokens.shape, BF16),
        jax.ShapeDtypeStruct(tokens.shape, BF16),
    ] + [jax.ShapeDtypeStruct((4, n), BF16) for n in PIECES]
    scratch = []
    for n in PIECES:
        scratch += piece_scratch(n)
    scratch += [
        pltpu.VMEM((WIDTH, 3 * INNER), BF16),
        pltpu.VMEM((INNER, WIDTH), BF16),
        pltpu.VMEM((WIDTH, 2 * HID), BF16),
        pltpu.VMEM((HID, WIDTH), BF16),
        pltpu.VMEM((2, 4, 3, HALF, INNER), BF16),
        pltpu.VMEM((4 * TOK, INNER), BF16),
        pltpu.VMEM((4 * TOK, INNER), BF16),
        pltpu.VMEM((TOK, KEYS), F32),
        pltpu.VMEM((4 * TOK, KEYS), F32),
        pltpu.VMEM((4 * TOK, KEYS), BF16),
        pltpu.VMEM((4 * TOK, KEYS), F32),
        pltpu.VMEM((4 * TOK, KEYS), BF16),
        pltpu.VMEM((4, TOK, INNER), F32),
        pltpu.VMEM((TOK, WIDTH), F32),
        pltpu.VMEM((TOK, WIDTH), F32),
        pltpu.VMEM((TOK, WIDTH), BF16),
        pltpu.VMEM((TOK, WIDTH), BF16),
        pltpu.VMEM((TOK, WIDTH), BF16),
        pltpu.VMEM((TOK, INNER), BF16),
        pltpu.VMEM((TOK, HID), F32),
        pltpu.VMEM((TOK, HID), BF16),
        pltpu.VMEM((TOK, 2 * HID), BF16),
        pltpu.VMEM((TOK, 3 * INNER), BF16),
        pltpu.VMEM((4, TOK, WIDTH), BF16),
        pltpu.VMEM((4, TOK, WIDTH), BF16),
        pltpu.VMEM((2, 2, 3, HALF, INNER), F32),
        pltpu.VMEM((2, 2, 3, HALF, INNER), BF16),
        pltpu.VMEM((2, 2, 3, HALF, INNER), BF16),
        pltpu.VMEM((2, 2, 2, HALF, INNER), BF16),
        pltpu.VMEM((2, 2, 2, HALF, INNER), BF16),
        pltpu.SemaphoreType.DMA((MESSAGES,)),
        pltpu.SemaphoreType.DMA((MESSAGES,)),
        pltpu.SemaphoreType.DMA((4,)),
    ]
    out, grad_input, gdown, gup, goq, gkv = pl.pallas_call(
        kernel,
        out_shape=out_shape,
        in_specs=[vmem] * 4
        + [pl.BlockSpec(memory_space=pltpu.SMEM)]
        + [anywhere] * 4,
        out_specs=[vmem] * 6,
        scratch_shapes=scratch,
        compiler_params=pltpu.CompilerParams(
            collective_id=0, has_side_effects=True, vmem_limit_bytes=58 * 1024 * 1024
        ),
    )(
        tokens,
        grad_output,
        attn_gain.reshape(1, width),
        mlp_gain.reshape(1, width),
        head_scale,
        w_qkv.reshape(width, 3 * INNER),
        w_out,
        w_up.reshape(width, 2 * HID),
        w_down,
    )
    grad_qkv = jnp.concatenate([goq[:, INNER:], gkv], axis=1).reshape(4, 3, INNER)
    return out, grad_input, grad_qkv, goq[:, :INNER], gup.reshape(4, 2, HID), gdown


def solution(mesh):
    placed = (
        P("row", "col", None),
        P("row", "col", None),
        P(),
        P(),
        P(None, None, "ch"),
        P("ch", None),
        P(None, None, "ch"),
        P("ch", None),
        P("ch"),
    )
    return jax.shard_map(
        shards,
        mesh=mesh,
        in_specs=placed,
        out_specs=(
            P("row", "col", None),
            P("row", "col", None),
            P(("row", "col"), None, "ch"),
            P(("row", "col"), "ch"),
            P(("row", "col"), None, "ch"),
            P(("row", "col"), "ch"),
        ),
        check_vma=False,
    )
```

```python
import jax
import jax.numpy as jnp
from jax import lax
from jax.experimental import pallas as pl
from jax.experimental.pallas import tpu as pltpu
from jax.sharding import PartitionSpec as P

HEADS = 8
RADIUS = 7
EPS = 1e-06
MESH = pl.DeviceIdType.MESH
F32 = jnp.float32
BF16 = jnp.bfloat16

TOK = 128
HALF = 64
KEYS = 768
WIDTH = 512
INNER = 256
HID = 1024
NROW, NCOL = 8, 16
NX, NZ = 4, 8


def nn(a, b):
    return lax.dot_general(a, b, (((1,), (0,)), ((), ())), preferred_element_type=F32)


def nt(a, b):
    return lax.dot_general(a, b, (((1,), (1,)), ((), ())), preferred_element_type=F32)


def tn(a, b):
    return lax.dot_general(a, b, (((0,), (0,)), ((), ())), preferred_element_type=F32)


def erf(x):
    return lax.erf(x)


def norm_scale(v):
    return lax.rsqrt(jnp.mean(v * v, axis=-1, keepdims=True) + EPS)


def norm_back(v, gain, upstream):
    s = norm_scale(v)
    n = v * s
    e = upstream * gain
    return s * (e - n * jnp.mean(e * n, axis=-1, keepdims=True))


def to_halves(block):
    return jnp.concatenate(
        [block[:, :8].reshape(HALF, WIDTH), block[:, 8:].reshape(HALF, WIDTH)], axis=0
    )


def from_halves(flat):
    return jnp.concatenate(
        [flat[:HALF].reshape(8, 8, WIDTH), flat[HALF:].reshape(8, 8, WIDTH)], axis=1
    )


class Links:
    def __init__(self, send, recv):
        self.send, self.recv, self.count, self.open = send, recv, 0, []

    def start(self, src, dst, device):
        copy = pltpu.make_async_remote_copy(
            src_ref=src,
            dst_ref=dst,
            send_sem=self.send.at[self.count],
            recv_sem=self.recv.at[self.count],
            device_id=device,
            device_id_type=MESH,
        )
        self.count += 1
        copy.start()
        self.open.append(copy)
        return copy

    def finish(self):
        for copy in self.open:
            copy.wait_send()


class Piece:
    def __init__(self, links, place, refs, out):
        self.links, self.place, self.out = links, place, out
        self.part, self.rc, self.xs, self.r1, self.s2, self.r2, self.ys, self.ry, self.zs, self.rz = refs

    def fill(self, left_t, right, at=0):
        wide = right.shape[1]
        for c in range(2):
            product = nn(left_t[c * 256 : (c + 1) * 256, :], right)
            self.part[c, :, at : at + wide] = product.astype(BF16)

    def core(self):
        core = self.place["core"]
        self.copy = self.links.start(
            self.part.at[1 - core], self.rc, self.place["core_peer"]
        )

    def x1(self):
        p = self.place
        self.copy.wait_recv()
        wide = self.part.shape[2] // 2
        for i in range(NX):
            rows = pl.ds(i * 64, 64)
            total = self.part[p["core"], rows, :].astype(F32) + self.rc[rows, :].astype(F32)
            total = total.astype(BF16)
            self.xs[0, i] = total[:, :wide]
            self.xs[1, i] = total[:, wide:]
        far = NX - 1 - p["x"]
        plan = (
            (0, 0, p["x_flip"], p["x_flip_peer"]),
            (1, 0, far, p["x_far_peer"]),
            (0, 1, p["x_both"], p["x_flip_peer"]),
            (1, 1, p["x_both"], p["x_far_peer"]),
        )
        self.copies = [
            self.links.start(self.xs.at[side, block], self.r1.at[side, order], peer)
            for side, order, block, peer in plan
        ]

    def x2(self):
        p = self.place
        for copy in self.copies:
            copy.wait_recv()
        far = NX - 1 - p["x"]
        self.copies = []
        for side, block, peer in ((0, far, p["x_far_peer"]), (1, p["x_flip"], p["x_flip_peer"])):
            total = self.xs[side, block].astype(F32) + self.r1[side, 1].astype(F32)
            self.s2[side] = total.astype(BF16)
            self.copies.append(self.links.start(self.s2.at[side], self.r2.at[side], peer))

    def y(self):
        p = self.place
        for copy in self.copies:
            copy.wait_recv()
        wide = self.part.shape[2] // 2
        for side in range(2):
            total = self.xs[side, p["x"]].astype(F32) + self.r1[side, 0].astype(F32)
            total = (total + self.r2[side].astype(F32)).astype(BF16)
            for half in range(2):
                self.ys[half, :, side * wide : (side + 1) * wide] = total[
                    half * 32 : half * 32 + 32
                ]
        self.copy = self.links.start(self.ys.at[1 - p["y"]], self.ry, p["y_peer"])

    def z(self):
        self.copy.wait_recv()
        self.z_of(self.ys[self.place["y"]].astype(F32) + self.ry[...].astype(F32))

    def z_of(self, total):
        p = self.place
        wide = total.shape[1] // 4
        for k in range(NZ):
            rows = total[4 * k : 4 * k + 4]
            block = jnp.concatenate(
                [rows[:, q * wide : (q + 1) * wide] for q in range(4)], axis=0
            )
            self.zs[k] = block.astype(BF16)
        self.copies = [
            self.links.start(
                self.zs.at[lax.rem(p["z"] + d, NZ)], self.rz.at[d - 1], p["z_peer"][d]
            )
            for d in range(1, NZ)
        ]

    def store(self):
        p = self.place
        for copy in self.copies:
            copy.wait_recv()
        total = self.zs[p["z"]].astype(F32)
        for d in range(NZ - 1):
            total = total + self.rz[d].astype(F32)
        wide = total.shape[1]
        for q in range(4):
            self.out[:, q * wide : (q + 1) * wide] = total[4 * q : 4 * q + 4].astype(BF16)


class LastPiece(Piece):
    def __init__(self, links, place, refs, out):
        self.links, self.place, self.out = links, place, out
        self.part, self.rc, self.xs, self.r1, self.zs, self.rz = refs

    def rows(self):
        p = self.place
        self.copy.wait_recv()
        for i in range(NROW):
            rows = pl.ds(i * 32, 32)
            total = self.part[p["core"], rows, :].astype(F32) + self.rc[rows, :].astype(F32)
            self.xs[i] = total.astype(BF16)
        self.copies = [
            self.links.start(
                self.xs.at[lax.rem(p["row"] + d, NROW)], self.r1.at[d - 1], p["row_peer"][d]
            )
            for d in range(1, NROW)
        ]

    def z(self):
        for copy in self.copies:
            copy.wait_recv()
        total = self.xs[self.place["row"]].astype(F32)
        for d in range(NROW - 1):
            total = total + self.r1[d].astype(F32)
        self.z_of(total)


PIECES = (1024, 2048, 512, 512)


def piece_scratch(n):
    return [
        pltpu.VMEM((2, 256, n), BF16),
        pltpu.VMEM((256, n), BF16),
        pltpu.VMEM((2, NX, 64, n // 2), BF16),
        pltpu.VMEM((2, 2, 64, n // 2), BF16),
        pltpu.VMEM((2, 64, n // 2), BF16),
        pltpu.VMEM((2, 64, n // 2), BF16),
        pltpu.VMEM((2, 32, n), BF16),
        pltpu.VMEM((32, n), BF16),
        pltpu.VMEM((NZ, 16, n // 4), BF16),
        pltpu.VMEM((NZ - 1, 16, n // 4), BF16),
    ]


def last_scratch(n):
    return [
        pltpu.VMEM((2, 256, n), BF16),
        pltpu.VMEM((256, n), BF16),
        pltpu.VMEM((NROW, 32, n), BF16),
        pltpu.VMEM((NROW - 1, 32, n), BF16),
        pltpu.VMEM((NZ, 16, n // 4), BF16),
        pltpu.VMEM((NZ - 1, 16, n // 4), BF16),
    ]


PER_PIECE = 10
PER_LAST = 6
MESSAGES = 96


def kernel(*refs):
    (tok, gout, attn_gain, mlp_gain, head_scale, wqkv_h, wout_h, wup_h, wdown_h) = refs[:9]
    (out_o, gin_o, gdown_o, gup_o, goq_o, gkv_o) = refs[9:15]
    refs = refs[15:]
    piece_refs = [refs[i * PER_PIECE : (i + 1) * PER_PIECE] for i in range(3)]
    refs = refs[3 * PER_PIECE :]
    last_refs = refs[:PER_LAST]
    (
        wqkv,
        wout,
        wup,
        wup_pairs,
        wdown,
        win,
        qmask,
        gmask,
        bias,
        probs,
        plow,
        dprob,
        dscore,
        raw,
        resid,
        gresid,
        ain,
        mlpin,
        fgrad,
        order,
        left_t,
        att,
        ghid,
        hidden,
        gmix,
        gproj,
        sums,
        sums_in,
        acc,
        rim_out,
        rim_in,
        ver_out,
        ver_in,
        send_sem,
        recv_sem,
        local_sem,
    ) = refs[PER_LAST:]

    row, col, ch = lax.axis_index("row"), lax.axis_index("col"), lax.axis_index("ch")
    x, y = row // 2, lax.rem(row, 2)
    z, core = col // 2, lax.rem(col, 2)
    above = (lax.rem(row + NROW - 1, NROW), col, ch)
    below = (lax.rem(row + 1, NROW), col, ch)
    left = (row, lax.rem(col + NCOL - 1, NCOL), ch)
    right = (row, lax.rem(col + 1, NCOL), ch)
    twin = (row, col, 1 - ch)
    x_flip = x + 1 - 2 * lax.rem(x, 2)
    row_peer = [(lax.rem(row + d, NROW), col, ch) for d in range(NROW)]
    z_peer = [(row, lax.rem(z + d, NZ) * 2 + core, ch) for d in range(NZ)]
    place = {
        "row": row,
        "x": x,
        "y": y,
        "z": z,
        "core": core,
        "x_flip": x_flip,
        "x_both": NX - 1 - x_flip,
        "x_flip_peer": (x_flip * 2 + y, col, ch),
        "x_far_peer": ((NX - 1 - x) * 2 + y, col, ch),
        "core_peer": (row, z * 2 + 1 - core, ch),
        "y_peer": (x * 2 + 1 - y, col, ch),
        "row_peer": row_peer,
        "z_peer": z_peer,
    }
    links = Links(send_sem, recv_sem)
    outs = (gdown_o, gup_o, goq_o)
    down_p, up_p, oq_p = [Piece(links, place, r, o) for r, o in zip(piece_refs, outs)]
    kv_p = LastPiece(links, place, last_refs, gkv_o)

    loads = []
    for i, (src, dst) in enumerate(
        ((wqkv_h, wqkv), (wdown_h, wdown), (wout_h, wout), (wup_h, wup_pairs))
    ):
        load = pltpu.make_async_copy(src, dst, local_sem.at[i])
        load.start()
        loads.append(load)

    barrier = pltpu.get_barrier_semaphore()
    peers = [left, right, twin] + row_peer[1:] + z_peer[1:]
    for peer in peers:
        pl.semaphore_signal(barrier, inc=1, device_id=peer, device_id_type=MESH)

    lane = lax.broadcasted_iota(jnp.int32, (1, INNER), 1) // 64
    same_head = (
        lax.broadcasted_iota(jnp.int32, (INNER, INNER), 0) // 64
        == lax.broadcasted_iota(jnp.int32, (INNER, INNER), 1) // 64
    )
    ones = jnp.where(same_head, 1.0, 0.0).astype(BF16)

    def head_sum(values):
        high = values.astype(BF16)
        low = (values - high.astype(F32)).astype(BF16)
        return nn(high, ones) + nn(low, ones)

    def head_rows(values):
        return [jnp.where(lane == h, values, jnp.zeros_like(values)) for h in range(4)]

    scale = jnp.zeros((1, INNER), F32)
    for h in range(4):
        scale = jnp.where(lane == h, head_scale[h], scale)

    toks = to_halves(tok[...].astype(F32))
    a = (toks * norm_scale(toks) * attn_gain[...]).astype(BF16)
    ain[...] = a
    fgrad[...] = to_halves(gout[...].astype(F32)).astype(BF16)
    loads[0].wait()
    key_raw = nn(a, wqkv[1])
    key_norm = lax.rsqrt(head_sum(key_raw * key_raw) + EPS)
    keys = (key_raw * key_norm).astype(BF16)
    win[0, 1, 1] = keys[:HALF]
    win[0, 2, 1] = keys[HALF:]
    raw[2] = key_raw
    raw[3] = key_norm
    pl.semaphore_wait(barrier, len(peers))

    def vertical(kv):
        return [
            links.start(win.at[kv, pl.ds(1, 2), 1], win.at[kv, pl.ds(1, 2), 0], below),
            links.start(win.at[kv, pl.ds(1, 2), 1], win.at[kv, pl.ds(1, 2), 2], above),
        ]

    def horizontal(kv, i):
        return [
            links.start(win.at[kv, 2, i], win.at[kv, 0, i], right),
            links.start(win.at[kv, 1, i], win.at[kv, 3, i], left),
        ]

    key_vert = vertical(0)
    key_side = horizontal(0, 1)
    values = nn(a, wqkv[2]).astype(BF16)
    win[1, 1, 1] = values[:HALF]
    win[1, 2, 1] = values[HALF:]
    value_vert = vertical(1)
    value_side = horizontal(1, 1)

    query_raw = nn(a, wqkv[0])
    query_norm = lax.rsqrt(head_sum(query_raw * query_raw) + EPS)
    raw[0] = query_raw
    raw[1] = query_norm
    queries = (query_raw * query_norm * scale).astype(BF16)
    for h, part in enumerate(head_rows(queries)):
        qmask[h * TOK : (h + 1) * TOK, :] = part

    def bias_rows(i, carry):
        t = lax.broadcasted_iota(jnp.int32, (32, KEYS), 0) + i * 32
        k = lax.broadcasted_iota(jnp.int32, (32, KEYS), 1)
        j = (
            jnp.where(k >= 192, 1, 0) + jnp.where(k >= 384, 1, 0) + jnp.where(k >= 576, 1, 0)
        )
        in_strip = k - 192 * j
        key_row = (in_strip >> 3) - 8
        key_col = (j - 1) * 8 + (k & 7)
        query_row = (t & 63) >> 3
        query_col = (t >> 6) * 8 + (t & 7)
        down, across_by = key_row - query_row, key_col - query_col
        at_row, at_col = row * 8 + key_row, col * 16 + key_col
        ok = (down >= -RADIUS) & (down <= RADIUS)
        ok = ok & (across_by >= -RADIUS) & (across_by <= RADIUS)
        ok = ok & (at_row >= 0) & (at_row < 8 * NROW) & (at_col >= 0) & (at_col < 16 * NCOL)
        bias[pl.ds(pl.multiple_of(i * 32, 32), 32), :] = jnp.where(ok, 0.0, -1e30)
        return carry

    lax.fori_loop(0, 4, bias_rows, 0)

    loads[3].wait()

    def part_rows(i, carry):
        rows = pl.ds(pl.multiple_of(i * 16, 16), 16)
        both = wup_pairs[rows].astype(F32)
        wup[rows, :HID] = both[:, 0, :].astype(BF16)
        wup[rows, HID:] = both[:, 1, :].astype(BF16)
        return carry

    lax.fori_loop(0, WIDTH // 16, part_rows, 0)

    at = lax.broadcasted_iota(jnp.int32, (WIDTH, WIDTH), 0)
    of = lax.broadcasted_iota(jnp.int32, (WIDTH, WIDTH), 1)
    to = ((of >> 2) & 1) * 256 + (of >> 3) * 4 + (of & 3)
    order[...] = jnp.where(at == to, 1.0, 0.0).astype(BF16)
    left_t[0] = nt(order[...], fgrad[...]).astype(BF16)
    left_t[1] = nt(order[...], ain[...]).astype(BF16)

    loads[1].wait()
    loads[2].wait()
    ghid[...] = nt(fgrad[...], wdown[...])

    for copy in key_vert:
        copy.wait_recv()
    key_side += horizontal(0, 0) + horizontal(0, 2)
    for copy in value_vert:
        copy.wait_recv()
    value_side += horizontal(1, 0) + horizontal(1, 2)
    for copy in key_side:
        copy.wait_recv()

    key_window = win[0].reshape(KEYS, INNER)
    probs[...] = nt(qmask[...], key_window)

    def softmax_rows(i, carry):
        rows = pl.ds(pl.multiple_of(i * 32, 32), 32)
        s = probs[rows, :] + bias[pl.ds(pl.multiple_of((i % 4) * 32, 32), 32), :]
        e = jnp.exp(s - jnp.max(s, axis=-1, keepdims=True))
        p = e * (1.0 / jnp.sum(e, axis=-1, keepdims=True))
        probs[rows, :] = p
        plow[rows, :] = p.astype(BF16)
        return carry

    lax.fori_loop(0, 16, softmax_rows, 0)
    for copy in value_side:
        copy.wait_recv()
    value_window = win[1].reshape(KEYS, INNER)

    def fold_heads(stacked):
        total = jnp.where(lane == 0, stacked[:TOK], 0.0)
        for h in range(1, 4):
            total = total + jnp.where(lane == h, stacked[h * TOK : (h + 1) * TOK], 0.0)
        return total

    attended = fold_heads(nn(plow[...], value_window)).astype(BF16)
    att[...] = attended

    def exchange(slot, value):
        sums[slot] = value.astype(BF16)
        return links.start(sums.at[slot], sums_in.at[slot], twin)

    def total_of(slot, copy):
        copy.wait_recv()
        return sums[slot].astype(F32) + sums_in[slot].astype(F32)

    attn_sum = exchange(0, nn(attended, wout[...]))
    residual = to_halves(tok[...].astype(F32)) + total_of(0, attn_sum)
    resid[...] = residual
    m = (residual * norm_scale(residual) * mlp_gain[...]).astype(BF16)
    mlpin[...] = m

    for j in range(4):
        cols = slice(j * 256, (j + 1) * 256)
        cols_v = slice(HID + j * 256, HID + (j + 1) * 256)
        gate = nn(m, wup[:, cols])
        val = nn(m, wup[:, cols_v])
        cdf = 0.5 * (1.0 + erf(gate * 0.7071067811865476))
        density = jnp.exp(-0.5 * gate * gate) * 0.3989422804014327
        act = gate * cdf
        hidden[:, cols] = (act * val).astype(BF16)
        gh = ghid[:, cols]
        gmix[:, cols] = (gh * val * (cdf + gate * density)).astype(BF16)
        gmix[:, cols_v] = (gh * act).astype(BF16)
    mlp_back = exchange(1, nt(gmix[...], wup[...]))
    mlp_sum = exchange(2, nn(hidden[...], wdown[...]))

    down_p.fill(left_t.at[0], hidden[...])
    down_p.core()
    left_t[2] = nt(order[...], mlpin[...]).astype(BF16)
    up_p.fill(left_t.at[2], gmix[...])
    up_p.core()
    down_p.x1()

    grad_resid = to_halves(gout[...].astype(F32)) + norm_back(
        resid[...], mlp_gain[...], total_of(1, mlp_back)
    )
    gresid[...] = grad_resid
    grad_low = grad_resid.astype(BF16)
    grad_att = nt(grad_low, wout[...]).astype(BF16)
    for h, part in enumerate(head_rows(grad_att)):
        gmask[h * TOK : (h + 1) * TOK, :] = part

    up_p.x1()

    def rims(kv, whole):
        whole = whole.reshape(4, 3, HALF, INNER)
        acc[kv] = whole[1:3]
        rim_out[kv, 0] = whole[0].astype(BF16)
        rim_out[kv, 1] = whole[3].astype(BF16)
        return [
            links.start(rim_out.at[kv, 0], rim_in.at[kv, 0], left),
            links.start(rim_out.at[kv, 1], rim_in.at[kv, 1], right),
        ]

    value_rims = rims(1, tn(plow[...], gmask[...]))
    down_p.x2()
    dprob[...] = nt(gmask[...], win[1].reshape(KEYS, INNER))

    def score_rows(i, carry):
        rows = pl.ds(pl.multiple_of(i * 32, 32), 32)
        p, g = probs[rows, :], dprob[rows, :]
        delta = jnp.sum(p * g, axis=-1, keepdims=True)
        dscore[rows, :] = (p * (g - delta)).astype(BF16)
        return carry

    lax.fori_loop(0, 16, score_rows, 0)
    key_rims = rims(0, tn(dscore[...], qmask[...]))

    def through_norm(which, incoming, factor):
        v, r = raw[2 * which], raw[2 * which + 1]
        along = head_sum(v * incoming)
        return factor * r * (incoming - r * r * v * along)

    grad_query = fold_heads(nn(dscore[...], win[0].reshape(KEYS, INNER)))
    gproj[:, :INNER] = through_norm(0, grad_query, scale).astype(BF16)
    left_t[3] = nt(order[...], gresid[...].astype(BF16)).astype(BF16)
    oq_p.fill(left_t.at[3], att[...])
    oq_p.fill(left_t.at[1], gproj[:, :INNER], INNER)
    oq_p.core()
    up_p.x2()

    def turn(kv, copies):
        for copy in copies:
            copy.wait_recv()
        acc[kv, 1] = acc[kv, 1] + rim_in[kv, 0].astype(F32)
        acc[kv, 0] = acc[kv, 0] + rim_in[kv, 1].astype(F32)
        ver_out[kv, 0] = acc[kv, :, 0].astype(BF16)
        ver_out[kv, 1] = acc[kv, :, 2].astype(BF16)
        return [
            links.start(ver_out.at[kv, 0], ver_in.at[kv, 0], above),
            links.start(ver_out.at[kv, 1], ver_in.at[kv, 1], below),
        ]

    value_turn = turn(1, value_rims)
    key_turn = turn(0, key_rims)
    down_p.y()
    out_o[...] = from_halves(resid[...] + total_of(2, mlp_sum)).astype(BF16)
    oq_p.x1()

    def owned(kv, copies):
        for copy in copies:
            copy.wait_recv()
        mine = acc[kv, :, 1] + ver_in[kv, 0].astype(F32) + ver_in[kv, 1].astype(F32)
        return mine.reshape(TOK, INNER)

    gproj[:, 2 * INNER :] = owned(1, value_turn).astype(BF16)
    gproj[:, INNER : 2 * INNER] = through_norm(1, owned(0, key_turn), 1.0).astype(BF16)
    back = nt(gproj[:, :INNER], wqkv[0]) + nt(gproj[:, INNER : 2 * INNER], wqkv[1])
    in_back = exchange(3, back + nt(gproj[:, 2 * INNER :], wqkv[2]))
    kv_p.fill(left_t.at[1], gproj[:, INNER:])
    kv_p.core()
    up_p.y()
    oq_p.x2()
    down_p.z()
    kv_p.rows()
    oq_p.y()
    grad_in = gresid[...] + norm_back(
        to_halves(tok[...].astype(F32)), attn_gain[...], total_of(3, in_back)
    )
    gin_o[...] = from_halves(grad_in).astype(BF16)
    up_p.z()
    oq_p.z()
    kv_p.z()
    down_p.store()
    up_p.store()
    oq_p.store()
    kv_p.store()
    links.finish()


def laid_out(out, gin, gdown, gup, goq, gkv, out_o, gin_o, gqkv_o, gout_o, gup_o, gdown_o):
    out_o[...] = out[...]
    gin_o[...] = gin[...]
    gdown_o[...] = gdown[...]
    gout_o[...] = goq[:, :INNER]
    gqkv_o[0] = goq[:, INNER:]
    gqkv_o[1] = gkv[:, :INNER]
    gqkv_o[2] = gkv[:, INNER:]
    both = gup[...].astype(F32)
    for r in range(4):
        pair = jnp.concatenate([both[r : r + 1, :HID], both[r : r + 1, HID:]], axis=0)
        gup_o[r] = pair.astype(BF16)


def shards(tokens, grad_output, attn_gain, mlp_gain, w_qkv, w_out, w_up, w_down, head_scale):
    rows, cols, width = tokens.shape
    vmem = pl.BlockSpec(memory_space=pltpu.VMEM)
    anywhere = pl.BlockSpec(memory_space=pl.ANY)
    out_shape = [
        jax.ShapeDtypeStruct(tokens.shape, BF16),
        jax.ShapeDtypeStruct(tokens.shape, BF16),
    ] + [jax.ShapeDtypeStruct((4, n), BF16) for n in PIECES]
    scratch = []
    for n in PIECES[:3]:
        scratch += piece_scratch(n)
    scratch += last_scratch(PIECES[3])
    scratch += [
        pltpu.VMEM((3, WIDTH, INNER), BF16),
        pltpu.VMEM((INNER, WIDTH), BF16),
        pltpu.VMEM((WIDTH, 2 * HID), BF16),
        pltpu.VMEM((WIDTH, 2, HID), BF16),
        pltpu.VMEM((HID, WIDTH), BF16),
        pltpu.VMEM((2, 4, 3, HALF, INNER), BF16),
        pltpu.VMEM((4 * TOK, INNER), BF16),
        pltpu.VMEM((4 * TOK, INNER), BF16),
        pltpu.VMEM((TOK, KEYS), F32),
        pltpu.VMEM((4 * TOK, KEYS), F32),
        pltpu.VMEM((4 * TOK, KEYS), BF16),
        pltpu.VMEM((4 * TOK, KEYS), F32),
        pltpu.VMEM((4 * TOK, KEYS), BF16),
        pltpu.VMEM((4, TOK, INNER), F32),
        pltpu.VMEM((TOK, WIDTH), F32),
        pltpu.VMEM((TOK, WIDTH), F32),
        pltpu.VMEM((TOK, WIDTH), BF16),
        pltpu.VMEM((TOK, WIDTH), BF16),
        pltpu.VMEM((TOK, WIDTH), BF16),
        pltpu.VMEM((WIDTH, WIDTH), BF16),
        pltpu.VMEM((4, WIDTH, TOK), BF16),
        pltpu.VMEM((TOK, INNER), BF16),
        pltpu.VMEM((TOK, HID), F32),
        pltpu.VMEM((TOK, HID), BF16),
        pltpu.VMEM((TOK, 2 * HID), BF16),
        pltpu.VMEM((TOK, 3 * INNER), BF16),
        pltpu.VMEM((4, TOK, WIDTH), BF16),
        pltpu.VMEM((4, TOK, WIDTH), BF16),
        pltpu.VMEM((2, 2, 3, HALF, INNER), F32),
        pltpu.VMEM((2, 2, 3, HALF, INNER), BF16),
        pltpu.VMEM((2, 2, 3, HALF, INNER), BF16),
        pltpu.VMEM((2, 2, 2, HALF, INNER), BF16),
        pltpu.VMEM((2, 2, 2, HALF, INNER), BF16),
        pltpu.SemaphoreType.DMA((MESSAGES,)),
        pltpu.SemaphoreType.DMA((MESSAGES,)),
        pltpu.SemaphoreType.DMA((4,)),
    ]
    out, grad_input, gdown, gup, goq, gkv = pl.pallas_call(
        kernel,
        out_shape=out_shape,
        in_specs=[vmem] * 4
        + [pl.BlockSpec(memory_space=pltpu.SMEM)]
        + [anywhere] * 4,
        out_specs=[vmem] * 6,
        scratch_shapes=scratch,
        compiler_params=pltpu.CompilerParams(
            collective_id=0, has_side_effects=True, vmem_limit_bytes=58 * 1024 * 1024
        ),
    )(
        tokens,
        grad_output,
        attn_gain.reshape(1, width),
        mlp_gain.reshape(1, width),
        head_scale,
        jnp.transpose(w_qkv, (1, 0, 2)),
        w_out,
        w_up,
        w_down,
    )
    out, grad_input, grad_qkv, grad_out_t, grad_up, grad_down_t = pl.pallas_call(
        laid_out,
        out_shape=[
            jax.ShapeDtypeStruct(tokens.shape, BF16),
            jax.ShapeDtypeStruct(tokens.shape, BF16),
            jax.ShapeDtypeStruct((3, 4, INNER), BF16),
            jax.ShapeDtypeStruct((4, INNER), BF16),
            jax.ShapeDtypeStruct((4, 2, HID), BF16),
            jax.ShapeDtypeStruct((4, HID), BF16),
        ],
        in_specs=[vmem] * 6,
        out_specs=[vmem] * 6,
    )(out, grad_input, gdown, gup, goq, gkv)
    return out, grad_input, jnp.transpose(grad_qkv, (1, 0, 2)), grad_out_t, grad_up, grad_down_t


def solution(mesh):
    placed = (
        P("row", "col", None),
        P("row", "col", None),
        P(),
        P(),
        P(None, None, "ch"),
        P("ch", None),
        P(None, None, "ch"),
        P("ch", None),
        P("ch"),
    )
    return jax.shard_map(
        shards,
        mesh=mesh,
        in_specs=placed,
        out_specs=(
            P("row", "col", None),
            P("row", "col", None),
            P(("row", "col"), None, "ch"),
            P(("row", "col"), "ch"),
            P(("row", "col"), None, "ch"),
            P(("row", "col"), "ch"),
        ),
        check_vma=False,
    )
```

```python
import jax
import jax.numpy as jnp
from jax import lax
from jax.experimental import pallas as pl
from jax.experimental.pallas import tpu as pltpu
from jax.sharding import PartitionSpec as P

HEADS = 8
RADIUS = 7
EPS = 1e-06
MESH = pl.DeviceIdType.MESH
F32 = jnp.float32
BF16 = jnp.bfloat16

TOK = 128
HALF = 64
KEYS = 768
WIDTH = 512
INNER = 256
HID = 1024
NROW, NCOL = 8, 16
NX, NZ = 4, 8


def nn(a, b):
    return lax.dot_general(a, b, (((1,), (0,)), ((), ())), preferred_element_type=F32)


def nt(a, b):
    return lax.dot_general(a, b, (((1,), (1,)), ((), ())), preferred_element_type=F32)


def tn(a, b):
    return lax.dot_general(a, b, (((0,), (0,)), ((), ())), preferred_element_type=F32)


def erf(x):
    return lax.erf(x)


def norm_scale(v):
    return lax.rsqrt(jnp.mean(v * v, axis=-1, keepdims=True) + EPS)


def norm_back(v, gain, upstream):
    s = norm_scale(v)
    n = v * s
    e = upstream * gain
    return s * (e - n * jnp.mean(e * n, axis=-1, keepdims=True))


def to_halves(block):
    return jnp.concatenate(
        [block[:, :8].reshape(HALF, WIDTH), block[:, 8:].reshape(HALF, WIDTH)], axis=0
    )


def from_halves(flat):
    return jnp.concatenate(
        [flat[:HALF].reshape(8, 8, WIDTH), flat[HALF:].reshape(8, 8, WIDTH)], axis=1
    )


class Links:
    def __init__(self, send, recv):
        self.send, self.recv, self.count, self.open = send, recv, 0, []

    def start(self, src, dst, device):
        copy = pltpu.make_async_remote_copy(
            src_ref=src,
            dst_ref=dst,
            send_sem=self.send.at[self.count],
            recv_sem=self.recv.at[self.count],
            device_id=device,
            device_id_type=MESH,
        )
        self.count += 1
        copy.start()
        self.open.append(copy)
        return copy

    def finish(self):
        for copy in self.open:
            copy.wait_send()


class Piece:
    def __init__(self, links, place, refs, out):
        self.links, self.place, self.out = links, place, out
        self.part, self.rc, self.xs, self.r1, self.s2, self.r2, self.ys, self.ry, self.zs, self.rz = refs

    def fill(self, left_t, right, at=0):
        wide = right.shape[1]
        for c in range(2):
            product = nn(left_t[c * 256 : (c + 1) * 256, :], right)
            self.part[c, :, at : at + wide] = product.astype(BF16)

    def core(self):
        core = self.place["core"]
        self.copy = self.links.start(
            self.part.at[1 - core], self.rc, self.place["core_peer"]
        )

    def x1(self):
        p = self.place
        self.copy.wait_recv()
        wide = self.part.shape[2] // 2
        for i in range(NX):
            rows = pl.ds(i * 64, 64)
            total = self.part[p["core"], rows, :].astype(F32) + self.rc[rows, :].astype(F32)
            total = total.astype(BF16)
            self.xs[0, i] = total[:, :wide]
            self.xs[1, i] = total[:, wide:]
        far = NX - 1 - p["x"]
        plan = (
            (0, 0, p["x_flip"], p["x_flip_peer"]),
            (1, 0, far, p["x_far_peer"]),
            (0, 1, p["x_both"], p["x_flip_peer"]),
            (1, 1, p["x_both"], p["x_far_peer"]),
        )
        self.copies = [
            self.links.start(self.xs.at[side, block], self.r1.at[side, order], peer)
            for side, order, block, peer in plan
        ]

    def x2(self):
        p = self.place
        for copy in self.copies:
            copy.wait_recv()
        far = NX - 1 - p["x"]
        self.copies = []
        for side, block, peer in ((0, far, p["x_far_peer"]), (1, p["x_flip"], p["x_flip_peer"])):
            total = self.xs[side, block].astype(F32) + self.r1[side, 1].astype(F32)
            self.s2[side] = total.astype(BF16)
            self.copies.append(self.links.start(self.s2.at[side], self.r2.at[side], peer))

    def y(self):
        p = self.place
        for copy in self.copies:
            copy.wait_recv()
        wide = self.part.shape[2] // 2
        for side in range(2):
            total = self.xs[side, p["x"]].astype(F32) + self.r1[side, 0].astype(F32)
            total = (total + self.r2[side].astype(F32)).astype(BF16)
            for half in range(2):
                self.ys[half, :, side * wide : (side + 1) * wide] = total[
                    half * 32 : half * 32 + 32
                ]
        self.copy = self.links.start(self.ys.at[1 - p["y"]], self.ry, p["y_peer"])

    def z(self):
        self.copy.wait_recv()
        self.z_of(self.ys[self.place["y"]].astype(F32) + self.ry[...].astype(F32))

    def z_of(self, total):
        p = self.place
        wide = total.shape[1] // 4
        for k in range(NZ):
            rows = total[4 * k : 4 * k + 4]
            block = jnp.concatenate(
                [rows[:, q * wide : (q + 1) * wide] for q in range(4)], axis=0
            )
            self.zs[k] = block.astype(BF16)
        self.copies = [
            self.links.start(
                self.zs.at[lax.rem(p["z"] + d, NZ)], self.rz.at[d - 1], p["z_peer"][d]
            )
            for d in range(1, NZ)
        ]

    def store(self):
        p = self.place
        for copy in self.copies:
            copy.wait_recv()
        total = self.zs[p["z"]].astype(F32)
        for d in range(NZ - 1):
            total = total + self.rz[d].astype(F32)
        wide = total.shape[1]
        for q in range(4):
            self.out[:, q * wide : (q + 1) * wide] = total[4 * q : 4 * q + 4].astype(BF16)


class LastPiece(Piece):
    def __init__(self, links, place, refs, out):
        self.links, self.place, self.out = links, place, out
        self.part, self.rc, self.xs, self.r1, self.zs, self.rz = refs

    def rows(self):
        p = self.place
        self.copy.wait_recv()
        for i in range(NROW):
            rows = pl.ds(i * 32, 32)
            total = self.part[p["core"], rows, :].astype(F32) + self.rc[rows, :].astype(F32)
            self.xs[i] = total.astype(BF16)
        self.copies = [
            self.links.start(
                self.xs.at[lax.rem(p["row"] + d, NROW)], self.r1.at[d - 1], p["row_peer"][d]
            )
            for d in range(1, NROW)
        ]

    def z(self):
        for copy in self.copies:
            copy.wait_recv()
        total = self.xs[self.place["row"]].astype(F32)
        for d in range(NROW - 1):
            total = total + self.r1[d].astype(F32)
        self.z_of(total)


PIECES = (1024, 2048, 512, 512)


def piece_scratch(n):
    return [
        pltpu.VMEM((2, 256, n), BF16),
        pltpu.VMEM((256, n), BF16),
        pltpu.VMEM((2, NX, 64, n // 2), BF16),
        pltpu.VMEM((2, 2, 64, n // 2), BF16),
        pltpu.VMEM((2, 64, n // 2), BF16),
        pltpu.VMEM((2, 64, n // 2), BF16),
        pltpu.VMEM((2, 32, n), BF16),
        pltpu.VMEM((32, n), BF16),
        pltpu.VMEM((NZ, 16, n // 4), BF16),
        pltpu.VMEM((NZ - 1, 16, n // 4), BF16),
    ]


def last_scratch(n):
    return [
        pltpu.VMEM((2, 256, n), BF16),
        pltpu.VMEM((256, n), BF16),
        pltpu.VMEM((NROW, 32, n), BF16),
        pltpu.VMEM((NROW - 1, 32, n), BF16),
        pltpu.VMEM((NZ, 16, n // 4), BF16),
        pltpu.VMEM((NZ - 1, 16, n // 4), BF16),
    ]


PER_PIECE = 10
PER_LAST = 6
MESSAGES = 96


def kernel(*refs):
    (tok, gout, attn_gain, mlp_gain, head_scale, wqkv_h, wout_h, wup_h, wdown_h) = refs[:9]
    (out_o, gin_o, gdown_o, gup_o, goq_o, gkv_o) = refs[9:15]
    refs = refs[15:]
    piece_refs = [refs[i * PER_PIECE : (i + 1) * PER_PIECE] for i in range(3)]
    refs = refs[3 * PER_PIECE :]
    last_refs = refs[:PER_LAST]
    (
        wqkv,
        wout,
        wup,
        wup_pairs,
        wdown,
        win,
        qmask,
        gmask,
        bias,
        probs,
        plow,
        dprob,
        dscore,
        raw,
        resid,
        gresid,
        ain,
        mlpin,
        fgrad,
        order,
        left_t,
        att,
        ghid,
        hidden,
        gmix,
        gproj,
        sums,
        sums_in,
        acc,
        rim_out,
        rim_in,
        ver_out,
        ver_in,
        send_sem,
        recv_sem,
        local_sem,
    ) = refs[PER_LAST:]

    row, col, ch = lax.axis_index("row"), lax.axis_index("col"), lax.axis_index("ch")
    x, y = row // 2, lax.rem(row, 2)
    z, core = col // 2, lax.rem(col, 2)
    above = (lax.rem(row + NROW - 1, NROW), col, ch)
    below = (lax.rem(row + 1, NROW), col, ch)
    left = (row, lax.rem(col + NCOL - 1, NCOL), ch)
    right = (row, lax.rem(col + 1, NCOL), ch)
    twin = (row, col, 1 - ch)
    x_flip = x + 1 - 2 * lax.rem(x, 2)
    row_peer = [(lax.rem(row + d, NROW), col, ch) for d in range(NROW)]
    z_peer = [(row, lax.rem(z + d, NZ) * 2 + core, ch) for d in range(NZ)]
    place = {
        "row": row,
        "x": x,
        "y": y,
        "z": z,
        "core": core,
        "x_flip": x_flip,
        "x_both": NX - 1 - x_flip,
        "x_flip_peer": (x_flip * 2 + y, col, ch),
        "x_far_peer": ((NX - 1 - x) * 2 + y, col, ch),
        "core_peer": (row, z * 2 + 1 - core, ch),
        "y_peer": (x * 2 + 1 - y, col, ch),
        "row_peer": row_peer,
        "z_peer": z_peer,
    }
    links = Links(send_sem, recv_sem)
    outs = (gdown_o, gup_o, goq_o)
    down_p, up_p, oq_p = [Piece(links, place, r, o) for r, o in zip(piece_refs, outs)]
    kv_p = LastPiece(links, place, last_refs, gkv_o)

    loads = []
    for i, (src, dst) in enumerate(
        ((wqkv_h, wqkv), (wup_h, wup_pairs), (wdown_h, wdown), (wout_h, wout))
    ):
        loads.append(pltpu.make_async_copy(src, dst, local_sem.at[i]))
    loads[0].start()

    barrier = pltpu.get_barrier_semaphore()
    peers = [left, right, twin] + row_peer[1:] + z_peer[1:]
    for peer in peers:
        pl.semaphore_signal(barrier, inc=1, device_id=peer, device_id_type=MESH)

    lane = lax.broadcasted_iota(jnp.int32, (1, INNER), 1) // 64
    same_head = (
        lax.broadcasted_iota(jnp.int32, (INNER, INNER), 0) // 64
        == lax.broadcasted_iota(jnp.int32, (INNER, INNER), 1) // 64
    )
    ones = jnp.where(same_head, 1.0, 0.0).astype(BF16)

    def head_sum(values):
        high = values.astype(BF16)
        low = (values - high.astype(F32)).astype(BF16)
        return nn(high, ones) + nn(low, ones)

    def head_rows(values):
        return [jnp.where(lane == h, values, jnp.zeros_like(values)) for h in range(4)]

    scale = jnp.zeros((1, INNER), F32)
    for h in range(4):
        scale = jnp.where(lane == h, head_scale[h], scale)

    toks = to_halves(tok[...].astype(F32))
    a = (toks * norm_scale(toks) * attn_gain[...]).astype(BF16)
    ain[...] = a
    fgrad[...] = to_halves(gout[...].astype(F32)).astype(BF16)
    loads[0].wait()
    for load in loads[1:]:
        load.start()
    key_raw = nn(a, wqkv[1])
    key_norm = lax.rsqrt(head_sum(key_raw * key_raw) + EPS)
    keys = (key_raw * key_norm).astype(BF16)
    win[0, 1, 1] = keys[:HALF]
    win[0, 2, 1] = keys[HALF:]
    raw[2] = key_raw
    raw[3] = key_norm
    pl.semaphore_wait(barrier, len(peers))

    def vertical(kv):
        return [
            links.start(win.at[kv, pl.ds(1, 2), 1], win.at[kv, pl.ds(1, 2), 0], below),
            links.start(win.at[kv, pl.ds(1, 2), 1], win.at[kv, pl.ds(1, 2), 2], above),
        ]

    def horizontal(kv, i):
        return [
            links.start(win.at[kv, 2, i], win.at[kv, 0, i], right),
            links.start(win.at[kv, 1, i], win.at[kv, 3, i], left),
        ]

    key_vert = vertical(0)
    key_side = horizontal(0, 1)
    values = nn(a, wqkv[2]).astype(BF16)
    win[1, 1, 1] = values[:HALF]
    win[1, 2, 1] = values[HALF:]
    value_vert = vertical(1)
    value_side = horizontal(1, 1)

    query_raw = nn(a, wqkv[0])
    query_norm = lax.rsqrt(head_sum(query_raw * query_raw) + EPS)
    raw[0] = query_raw
    raw[1] = query_norm
    queries = (query_raw * query_norm * scale).astype(BF16)
    for h, part in enumerate(head_rows(queries)):
        qmask[h * TOK : (h + 1) * TOK, :] = part

    def bias_rows(i, carry):
        t = lax.broadcasted_iota(jnp.int32, (32, KEYS), 0) + i * 32
        k = lax.broadcasted_iota(jnp.int32, (32, KEYS), 1)
        j = (
            jnp.where(k >= 192, 1, 0) + jnp.where(k >= 384, 1, 0) + jnp.where(k >= 576, 1, 0)
        )
        in_strip = k - 192 * j
        key_row = (in_strip >> 3) - 8
        key_col = (j - 1) * 8 + (k & 7)
        query_row = (t & 63) >> 3
        query_col = (t >> 6) * 8 + (t & 7)
        down, across_by = key_row - query_row, key_col - query_col
        at_row, at_col = row * 8 + key_row, col * 16 + key_col
        ok = (down >= -RADIUS) & (down <= RADIUS)
        ok = ok & (across_by >= -RADIUS) & (across_by <= RADIUS)
        ok = ok & (at_row >= 0) & (at_row < 8 * NROW) & (at_col >= 0) & (at_col < 16 * NCOL)
        bias[pl.ds(pl.multiple_of(i * 32, 32), 32), :] = jnp.where(ok, 0.0, -1e30)
        return carry

    lax.fori_loop(0, 4, bias_rows, 0)

    def part_rows(i, carry):
        rows = pl.ds(pl.multiple_of(i * 32, 32), 32)
        both = wup_pairs[rows]
        wup[rows, :HID] = both[:, 0, :]
        wup[rows, HID:] = both[:, 1, :]
        return carry

    loads[1].wait()
    lax.fori_loop(0, 8, part_rows, 0)
    for copy in key_vert:
        copy.wait_recv()
    key_side += horizontal(0, 0) + horizontal(0, 2)
    lax.fori_loop(8, 16, part_rows, 0)
    for copy in key_side:
        copy.wait_recv()

    key_window = win[0].reshape(KEYS, INNER)
    probs[...] = nt(qmask[...], key_window)
    for copy in value_vert:
        copy.wait_recv()
    value_side += horizontal(1, 0) + horizontal(1, 2)

    for i in range(16):
        rows = pl.ds(i * 32, 32)
        s = probs[rows, :] + bias[pl.ds((i % 4) * 32, 32), :]
        e = jnp.exp(s - jnp.max(s, axis=-1, keepdims=True))
        p = e * (1.0 / jnp.sum(e, axis=-1, keepdims=True))
        probs[rows, :] = p
        plow[rows, :] = p.astype(BF16)
    at = lax.broadcasted_iota(jnp.int32, (WIDTH, WIDTH), 0)
    of = lax.broadcasted_iota(jnp.int32, (WIDTH, WIDTH), 1)
    to = ((of >> 2) & 1) * 256 + (of >> 3) * 4 + (of & 3)
    order[...] = jnp.where(at == to, 1.0, 0.0).astype(BF16)
    left_t[0] = nt(order[...], fgrad[...]).astype(BF16)
    left_t[1] = nt(order[...], ain[...]).astype(BF16)

    loads[2].wait()
    loads[3].wait()
    ghid[...] = nt(fgrad[...], wdown[...])

    for copy in value_side:
        copy.wait_recv()
    value_window = win[1].reshape(KEYS, INNER)

    def fold_heads(stacked):
        total = jnp.where(lane == 0, stacked[:TOK], 0.0)
        for h in range(1, 4):
            total = total + jnp.where(lane == h, stacked[h * TOK : (h + 1) * TOK], 0.0)
        return total

    attended = fold_heads(nn(plow[...], value_window)).astype(BF16)
    att[...] = attended

    def exchange(slot, product):
        copies = []
        for half in range(2):
            sums[slot, half] = product(slice(half * INNER, (half + 1) * INNER)).astype(BF16)
            copies.append(links.start(sums.at[slot, half], sums_in.at[slot, half], twin))
        return copies

    def total_of(slot, copies):
        for copy in copies:
            copy.wait_recv()
        halves = [sums[slot, i].astype(F32) + sums_in[slot, i].astype(F32) for i in range(2)]
        return jnp.concatenate(halves, axis=1)

    attn_sum = exchange(0, lambda c: nn(attended, wout[:, c]))
    residual = to_halves(tok[...].astype(F32)) + total_of(0, attn_sum)
    resid[...] = residual
    m = (residual * norm_scale(residual) * mlp_gain[...]).astype(BF16)
    mlpin[...] = m

    for j in range(4):
        cols = slice(j * 256, (j + 1) * 256)
        cols_v = slice(HID + j * 256, HID + (j + 1) * 256)
        gate = nn(m, wup[:, cols])
        val = nn(m, wup[:, cols_v])
        cdf = 0.5 * (1.0 + erf(gate * 0.7071067811865476))
        density = jnp.exp(-0.5 * gate * gate) * 0.3989422804014327
        act = gate * cdf
        hidden[:, cols] = (act * val).astype(BF16)
        gh = ghid[:, cols]
        gmix[:, cols] = (gh * val * (cdf + gate * density)).astype(BF16)
        gmix[:, cols_v] = (gh * act).astype(BF16)
    mlp_back = exchange(1, lambda c: nt(gmix[...], wup[c, :]))

    down_p.fill(left_t.at[0], hidden[...])
    down_p.core()
    left_t[2] = nt(order[...], mlpin[...]).astype(BF16)
    up_p.fill(left_t.at[2], gmix[...])
    up_p.core()
    down_p.x1()

    grad_resid = to_halves(gout[...].astype(F32)) + norm_back(
        resid[...], mlp_gain[...], total_of(1, mlp_back)
    )
    gresid[...] = grad_resid
    grad_low = grad_resid.astype(BF16)
    grad_att = nt(grad_low, wout[...]).astype(BF16)
    for h, part in enumerate(head_rows(grad_att)):
        gmask[h * TOK : (h + 1) * TOK, :] = part

    def rims(kv, whole):
        whole = whole.reshape(4, 3, HALF, INNER)
        acc[kv] = whole[1:3]
        rim_out[kv, 0] = whole[0].astype(BF16)
        rim_out[kv, 1] = whole[3].astype(BF16)
        return [
            links.start(rim_out.at[kv, 0], rim_in.at[kv, 0], left),
            links.start(rim_out.at[kv, 1], rim_in.at[kv, 1], right),
        ]

    value_rims = rims(1, tn(plow[...], gmask[...]))
    up_p.x1()
    mlp_sum = exchange(2, lambda c: nn(hidden[...], wdown[:, c]))
    dprob[...] = nt(gmask[...], win[1].reshape(KEYS, INNER))

    for i in range(16):
        rows = pl.ds(i * 32, 32)
        p, g = probs[rows, :], dprob[rows, :]
        delta = jnp.sum(p * g, axis=-1, keepdims=True)
        dscore[rows, :] = (p * (g - delta)).astype(BF16)

    key_rims = rims(0, tn(dscore[...], qmask[...]))
    down_p.x2()

    def through_norm(which, incoming, factor):
        v, r = raw[2 * which], raw[2 * which + 1]
        along = head_sum(v * incoming)
        return factor * r * (incoming - r * r * v * along)

    grad_query = fold_heads(nn(dscore[...], win[0].reshape(KEYS, INNER)))
    gproj[:, :INNER] = through_norm(0, grad_query, scale).astype(BF16)
    left_t[3] = nt(order[...], gresid[...].astype(BF16)).astype(BF16)
    oq_p.fill(left_t.at[3], att[...])
    oq_p.fill(left_t.at[1], gproj[:, :INNER], INNER)
    oq_p.core()

    def turn(kv, copies):
        for copy in copies:
            copy.wait_recv()
        acc[kv, 1] = acc[kv, 1] + rim_in[kv, 0].astype(F32)
        acc[kv, 0] = acc[kv, 0] + rim_in[kv, 1].astype(F32)
        ver_out[kv, 0] = acc[kv, :, 0].astype(BF16)
        ver_out[kv, 1] = acc[kv, :, 2].astype(BF16)
        return [
            links.start(ver_out.at[kv, 0], ver_in.at[kv, 0], above),
            links.start(ver_out.at[kv, 1], ver_in.at[kv, 1], below),
        ]

    value_turn = turn(1, value_rims)
    key_turn = turn(0, key_rims)
    up_p.x2()
    down_p.y()
    out_o[...] = from_halves(resid[...] + total_of(2, mlp_sum)).astype(BF16)
    oq_p.x1()

    def owned(kv, copies):
        for copy in copies:
            copy.wait_recv()
        mine = acc[kv, :, 1] + ver_in[kv, 0].astype(F32) + ver_in[kv, 1].astype(F32)
        return mine.reshape(TOK, INNER)

    gproj[:, 2 * INNER :] = owned(1, value_turn).astype(BF16)
    gproj[:, INNER : 2 * INNER] = through_norm(1, owned(0, key_turn), 1.0).astype(BF16)
    kv_p.fill(left_t.at[1], gproj[:, INNER:])
    kv_p.core()

    def in_part(c):
        part = nt(gproj[:, :INNER], wqkv[0, c, :])
        part = part + nt(gproj[:, INNER : 2 * INNER], wqkv[1, c, :])
        return part + nt(gproj[:, 2 * INNER :], wqkv[2, c, :])

    in_back = exchange(3, in_part)
    up_p.y()
    oq_p.x2()
    kv_p.rows()
    down_p.z()
    oq_p.y()
    grad_in = gresid[...] + norm_back(
        to_halves(tok[...].astype(F32)), attn_gain[...], total_of(3, in_back)
    )
    gin_o[...] = from_halves(grad_in).astype(BF16)
    up_p.z()
    kv_p.z()
    oq_p.z()
    down_p.store()
    up_p.store()
    oq_p.store()
    kv_p.store()
    links.finish()


def laid_out(out, gin, gdown, gup, goq, gkv, out_o, gin_o, gqkv_o, gout_o, gup_o, gdown_o):
    out_o[...] = out[...]
    gin_o[...] = gin[...]
    gdown_o[...] = gdown[...]
    gout_o[...] = goq[:, :INNER]
    gqkv_o[0] = goq[:, INNER:]
    gqkv_o[1] = gkv[:, :INNER]
    gqkv_o[2] = gkv[:, INNER:]
    both = gup[...].astype(F32)
    for r in range(4):
        pair = jnp.concatenate([both[r : r + 1, :HID], both[r : r + 1, HID:]], axis=0)
        gup_o[r] = pair.astype(BF16)


def shards(tokens, grad_output, attn_gain, mlp_gain, w_qkv, w_out, w_up, w_down, head_scale):
    rows, cols, width = tokens.shape
    vmem = pl.BlockSpec(memory_space=pltpu.VMEM)
    anywhere = pl.BlockSpec(memory_space=pl.ANY)
    out_shape = [
        jax.ShapeDtypeStruct(tokens.shape, BF16),
        jax.ShapeDtypeStruct(tokens.shape, BF16),
    ] + [jax.ShapeDtypeStruct((4, n), BF16) for n in PIECES]
    scratch = []
    for n in PIECES[:3]:
        scratch += piece_scratch(n)
    scratch += last_scratch(PIECES[3])
    scratch += [
        pltpu.VMEM((3, WIDTH, INNER), BF16),
        pltpu.VMEM((INNER, WIDTH), BF16),
        pltpu.VMEM((WIDTH, 2 * HID), BF16),
        pltpu.VMEM((WIDTH, 2, HID), BF16),
        pltpu.VMEM((HID, WIDTH), BF16),
        pltpu.VMEM((2, 4, 3, HALF, INNER), BF16),
        pltpu.VMEM((4 * TOK, INNER), BF16),
        pltpu.VMEM((4 * TOK, INNER), BF16),
        pltpu.VMEM((TOK, KEYS), F32),
        pltpu.VMEM((4 * TOK, KEYS), F32),
        pltpu.VMEM((4 * TOK, KEYS), BF16),
        pltpu.VMEM((4 * TOK, KEYS), F32),
        pltpu.VMEM((4 * TOK, KEYS), BF16),
        pltpu.VMEM((4, TOK, INNER), F32),
        pltpu.VMEM((TOK, WIDTH), F32),
        pltpu.VMEM((TOK, WIDTH), F32),
        pltpu.VMEM((TOK, WIDTH), BF16),
        pltpu.VMEM((TOK, WIDTH), BF16),
        pltpu.VMEM((TOK, WIDTH), BF16),
        pltpu.VMEM((WIDTH, WIDTH), BF16),
        pltpu.VMEM((4, WIDTH, TOK), BF16),
        pltpu.VMEM((TOK, INNER), BF16),
        pltpu.VMEM((TOK, HID), F32),
        pltpu.VMEM((TOK, HID), BF16),
        pltpu.VMEM((TOK, 2 * HID), BF16),
        pltpu.VMEM((TOK, 3 * INNER), BF16),
        pltpu.VMEM((4, 2, TOK, INNER), BF16),
        pltpu.VMEM((4, 2, TOK, INNER), BF16),
        pltpu.VMEM((2, 2, 3, HALF, INNER), F32),
        pltpu.VMEM((2, 2, 3, HALF, INNER), BF16),
        pltpu.VMEM((2, 2, 3, HALF, INNER), BF16),
        pltpu.VMEM((2, 2, 2, HALF, INNER), BF16),
        pltpu.VMEM((2, 2, 2, HALF, INNER), BF16),
        pltpu.SemaphoreType.DMA((MESSAGES,)),
        pltpu.SemaphoreType.DMA((MESSAGES,)),
        pltpu.SemaphoreType.DMA((4,)),
    ]
    out, grad_input, gdown, gup, goq, gkv = pl.pallas_call(
        kernel,
        out_shape=out_shape,
        in_specs=[vmem] * 4
        + [pl.BlockSpec(memory_space=pltpu.SMEM)]
        + [anywhere] * 4,
        out_specs=[vmem] * 6,
        scratch_shapes=scratch,
        compiler_params=pltpu.CompilerParams(
            collective_id=0, has_side_effects=True, vmem_limit_bytes=58 * 1024 * 1024
        ),
    )(
        tokens,
        grad_output,
        attn_gain.reshape(1, width),
        mlp_gain.reshape(1, width),
        head_scale,
        jnp.transpose(w_qkv, (1, 0, 2)),
        w_out,
        w_up,
        w_down,
    )
    out, grad_input, grad_qkv, grad_out_t, grad_up, grad_down_t = pl.pallas_call(
        laid_out,
        out_shape=[
            jax.ShapeDtypeStruct(tokens.shape, BF16),
            jax.ShapeDtypeStruct(tokens.shape, BF16),
            jax.ShapeDtypeStruct((3, 4, INNER), BF16),
            jax.ShapeDtypeStruct((4, INNER), BF16),
            jax.ShapeDtypeStruct((4, 2, HID), BF16),
            jax.ShapeDtypeStruct((4, HID), BF16),
        ],
        in_specs=[vmem] * 6,
        out_specs=[vmem] * 6,
    )(out, grad_input, gdown, gup, goq, gkv)
    return out, grad_input, jnp.transpose(grad_qkv, (1, 0, 2)), grad_out_t, grad_up, grad_down_t


def solution(mesh):
    placed = (
        P("row", "col", None),
        P("row", "col", None),
        P(),
        P(),
        P(None, None, "ch"),
        P("ch", None),
        P(None, None, "ch"),
        P("ch", None),
        P("ch"),
    )
    return jax.shard_map(
        shards,
        mesh=mesh,
        in_specs=placed,
        out_specs=(
            P("row", "col", None),
            P("row", "col", None),
            P(("row", "col"), None, "ch"),
            P(("row", "col"), "ch"),
            P(("row", "col"), None, "ch"),
            P(("row", "col"), "ch"),
        ),
        check_vma=False,
    )
```

```python
import jax
import jax.numpy as jnp
from jax import lax
from jax.experimental import pallas as pl
from jax.experimental.pallas import tpu as pltpu
from jax.sharding import PartitionSpec as P

HEADS = 8
RADIUS = 7
EPS = 1e-06
MESH = pl.DeviceIdType.MESH
F32 = jnp.float32
BF16 = jnp.bfloat16

TOK = 128
HALF = 64
KEYS = 768
WIDTH = 512
INNER = 256
HID = 1024
NROW, NCOL = 8, 16
NX, NZ = 4, 8


def nn(a, b):
    return lax.dot_general(a, b, (((1,), (0,)), ((), ())), preferred_element_type=F32)


def nt(a, b):
    return lax.dot_general(a, b, (((1,), (1,)), ((), ())), preferred_element_type=F32)


def tn(a, b):
    return lax.dot_general(a, b, (((0,), (0,)), ((), ())), preferred_element_type=F32)


def erf(x):
    return lax.erf(x)


def norm_scale(v):
    return lax.rsqrt(jnp.mean(v * v, axis=-1, keepdims=True) + EPS)


def norm_back(v, gain, upstream):
    s = norm_scale(v)
    n = v * s
    e = upstream * gain
    return s * (e - n * jnp.mean(e * n, axis=-1, keepdims=True))


def to_halves(block):
    return jnp.concatenate(
        [block[:, :8].reshape(HALF, WIDTH), block[:, 8:].reshape(HALF, WIDTH)], axis=0
    )


def from_halves(flat):
    return jnp.concatenate(
        [flat[:HALF].reshape(8, 8, WIDTH), flat[HALF:].reshape(8, 8, WIDTH)], axis=1
    )


class Links:
    def __init__(self, send, recv):
        self.send, self.recv, self.count, self.open = send, recv, 0, []

    def start(self, src, dst, device):
        copy = pltpu.make_async_remote_copy(
            src_ref=src,
            dst_ref=dst,
            send_sem=self.send.at[self.count],
            recv_sem=self.recv.at[self.count],
            device_id=device,
            device_id_type=MESH,
        )
        self.count += 1
        copy.start()
        self.open.append(copy)
        return copy

    def finish(self):
        for copy in self.open:
            copy.wait_send()


class Piece:
    def __init__(self, links, place, refs, out):
        self.links, self.place, self.out = links, place, out
        self.part, self.rc, self.xs, self.r1, self.s2, self.r2, self.ys, self.ry, self.zs, self.rz = refs

    def fill(self, left_t, right, at=0):
        wide = right.shape[1]
        for c in range(2):
            product = nn(left_t[c * 256 : (c + 1) * 256, :], right)
            self.part[c, :, at : at + wide] = product.astype(BF16)

    def core(self):
        core = self.place["core"]
        self.copy = self.links.start(
            self.part.at[1 - core], self.rc, self.place["core_peer"]
        )

    def x1(self):
        p = self.place
        self.copy.wait_recv()
        wide = self.part.shape[2] // 2
        for i in range(NX):
            rows = pl.ds(i * 64, 64)
            total = self.part[p["core"], rows, :].astype(F32) + self.rc[rows, :].astype(F32)
            total = total.astype(BF16)
            self.xs[0, i] = total[:, :wide]
            self.xs[1, i] = total[:, wide:]
        far = NX - 1 - p["x"]
        plan = (
            (0, 0, p["x_flip"], p["x_flip_peer"]),
            (1, 0, far, p["x_far_peer"]),
            (0, 1, p["x_both"], p["x_flip_peer"]),
            (1, 1, p["x_both"], p["x_far_peer"]),
        )
        self.copies = [
            self.links.start(self.xs.at[side, block], self.r1.at[side, order], peer)
            for side, order, block, peer in plan
        ]

    def x2(self):
        p = self.place
        for copy in self.copies:
            copy.wait_recv()
        far = NX - 1 - p["x"]
        self.copies = []
        for side, block, peer in ((0, far, p["x_far_peer"]), (1, p["x_flip"], p["x_flip_peer"])):
            total = self.xs[side, block].astype(F32) + self.r1[side, 1].astype(F32)
            self.s2[side] = total.astype(BF16)
            self.copies.append(self.links.start(self.s2.at[side], self.r2.at[side], peer))

    def z(self):
        p = self.place
        for copy in self.copies:
            copy.wait_recv()
        wide = self.part.shape[2] // 2
        for side in range(2):
            total = self.xs[side, p["x"]].astype(F32) + self.r1[side, 0].astype(F32)
            total = (total + self.r2[side].astype(F32)).astype(BF16)
            for k in range(NZ):
                self.zs[k, side * 8 : side * 8 + 8, :] = total[8 * k : 8 * k + 8]
        self.copies = [
            self.links.start(
                self.zs.at[lax.rem(p["z"] + d, NZ)], self.rz.at[d - 1], p["z_peer"][d]
            )
            for d in range(1, NZ)
        ]

    def y(self):
        p = self.place
        for copy in self.copies:
            copy.wait_recv()
        total = self.zs[p["z"]].astype(F32)
        for d in range(NZ - 1):
            total = total + self.rz[d].astype(F32)
        wide = total.shape[1] // 2
        for k in range(2):
            quarters = [
                total[8 * h + 4 * k : 8 * h + 4 * k + 4, q * wide : (q + 1) * wide]
                for h in range(2)
                for q in range(2)
            ]
            self.ys[k] = jnp.concatenate(quarters, axis=0).astype(BF16)
        self.copy = self.links.start(self.ys.at[1 - p["y"]], self.ry, p["y_peer"])

    def store(self):
        self.copy.wait_recv()
        self.write(self.ys[self.place["y"]].astype(F32) + self.ry[...].astype(F32))

    def write(self, total):
        wide = total.shape[1]
        for q in range(4):
            self.out[:, q * wide : (q + 1) * wide] = total[4 * q : 4 * q + 4].astype(BF16)


class LastPiece(Piece):
    def __init__(self, links, place, refs, out):
        self.links, self.place, self.out = links, place, out
        self.part, self.rc, self.xs, self.r1, self.zs, self.rz = refs
        self.core_copies, self.copies = [None, None], []

    def core(self, k, left_t, right):
        core = self.place["core"]
        for c in range(2):
            product = nn(left_t[c * 256 : (c + 1) * 256, :], right)
            self.part[k, c] = product.astype(BF16)
        self.core_copies[k] = self.links.start(
            self.part.at[k, 1 - core], self.rc.at[k], self.place["core_peer"]
        )

    def x(self, k):
        p = self.place
        self.core_copies[k].wait_recv()
        for i in range(NX):
            rows = pl.ds(i * 64, 64)
            total = self.part[k, p["core"], rows, :].astype(F32)
            self.xs[k, i] = (total + self.rc[k, rows, :].astype(F32)).astype(BF16)
        self.copies += [
            self.links.start(
                self.xs.at[k, lax.rem(p["x"] + d, NX)], self.r1.at[k, d - 1], p["x_peer"][d]
            )
            for d in range(1, NX)
        ]

    def zy(self):
        p = self.place
        for copy in self.copies:
            copy.wait_recv()
        totals = []
        for k in range(2):
            total = self.xs[k, p["x"]].astype(F32)
            for d in range(NX - 1):
                total = total + self.r1[k, d].astype(F32)
            totals.append(total)
        for block in range(2 * NZ):
            quarters = [
                total[4 * block : 4 * block + 4, q * 128 : (q + 1) * 128]
                for total in totals
                for q in range(2)
            ]
            self.zs[block] = jnp.concatenate(quarters, axis=0).astype(BF16)
        self.copies = []
        for d in range(1, 2 * NZ):
            to_z, to_y = lax.rem(p["z"] + d // 2, NZ), lax.rem(p["y"] + d % 2, 2)
            self.copies.append(
                self.links.start(
                    self.zs.at[to_z * 2 + to_y], self.rz.at[d - 1], p["zy_peer"][d]
                )
            )

    def store(self):
        p = self.place
        for copy in self.copies:
            copy.wait_recv()
        total = self.zs[p["z"] * 2 + p["y"]].astype(F32)
        for d in range(2 * NZ - 1):
            total = total + self.rz[d].astype(F32)
        self.write(total)


PIECES = (1024, 2048, 512, 512)


def piece_scratch(n):
    return [
        pltpu.VMEM((2, 256, n), BF16),
        pltpu.VMEM((256, n), BF16),
        pltpu.VMEM((2, NX, 64, n // 2), BF16),
        pltpu.VMEM((2, 2, 64, n // 2), BF16),
        pltpu.VMEM((2, 64, n // 2), BF16),
        pltpu.VMEM((2, 64, n // 2), BF16),
        pltpu.VMEM((2, 16, n // 4), BF16),
        pltpu.VMEM((16, n // 4), BF16),
        pltpu.VMEM((NZ, 16, n // 2), BF16),
        pltpu.VMEM((NZ - 1, 16, n // 2), BF16),
    ]


def last_scratch(n):
    return [
        pltpu.VMEM((2, 2, 256, n // 2), BF16),
        pltpu.VMEM((2, 256, n // 2), BF16),
        pltpu.VMEM((2, NX, 64, n // 2), BF16),
        pltpu.VMEM((2, NX - 1, 64, n // 2), BF16),
        pltpu.VMEM((2 * NZ, 16, n // 4), BF16),
        pltpu.VMEM((2 * NZ - 1, 16, n // 4), BF16),
    ]


PER_PIECE = 10
PER_LAST = 6
MESSAGES = 104


def kernel(*refs):
    (tok, gout, attn_gain, mlp_gain, head_scale, wqkv_h, wout_h, wup_h, wdown_h) = refs[:9]
    (out_o, gin_o, gdown_o, gup_o, goq_o, gkv_o) = refs[9:15]
    refs = refs[15:]
    piece_refs = [refs[i * PER_PIECE : (i + 1) * PER_PIECE] for i in range(3)]
    refs = refs[3 * PER_PIECE :]
    last_refs = refs[:PER_LAST]
    (
        wqkv,
        wout,
        wup,
        wup_pairs,
        wdown,
        win,
        qmask,
        gmask,
        bias,
        probs,
        plow,
        dprob,
        dscore,
        raw,
        resid,
        gresid,
        ain,
        mlpin,
        fgrad,
        order,
        left_t,
        att,
        ghid,
        hidden,
        gmix,
        gproj,
        sums,
        sums_in,
        acc,
        rim_out,
        rim_in,
        ver_out,
        ver_in,
        send_sem,
        recv_sem,
        local_sem,
    ) = refs[PER_LAST:]

    row, col, ch = lax.axis_index("row"), lax.axis_index("col"), lax.axis_index("ch")
    x, y = row // 2, lax.rem(row, 2)
    z, core = col // 2, lax.rem(col, 2)
    above = (lax.rem(row + NROW - 1, NROW), col, ch)
    below = (lax.rem(row + 1, NROW), col, ch)
    left = (row, lax.rem(col + NCOL - 1, NCOL), ch)
    right = (row, lax.rem(col + 1, NCOL), ch)
    twin = (row, col, 1 - ch)
    x_flip = x + 1 - 2 * lax.rem(x, 2)
    x_peer = [(lax.rem(x + d, NX) * 2 + y, col, ch) for d in range(NX)]
    z_peer = [(row, lax.rem(z + d, NZ) * 2 + core, ch) for d in range(NZ)]
    zy_peer = [
        (x * 2 + lax.rem(y + d % 2, 2), lax.rem(z + d // 2, NZ) * 2 + core, ch)
        for d in range(2 * NZ)
    ]
    place = {
        "x": x,
        "y": y,
        "z": z,
        "core": core,
        "x_flip": x_flip,
        "x_both": NX - 1 - x_flip,
        "x_flip_peer": (x_flip * 2 + y, col, ch),
        "x_far_peer": ((NX - 1 - x) * 2 + y, col, ch),
        "core_peer": (row, z * 2 + 1 - core, ch),
        "y_peer": (x * 2 + 1 - y, col, ch),
        "x_peer": x_peer,
        "zy_peer": zy_peer,
        "z_peer": z_peer,
    }
    links = Links(send_sem, recv_sem)
    outs = (gdown_o, gup_o, goq_o)
    down_p, up_p, oq_p = [Piece(links, place, r, o) for r, o in zip(piece_refs, outs)]
    kv_p = LastPiece(links, place, last_refs, gkv_o)

    loads = []
    for i, (src, dst) in enumerate(
        ((wqkv_h, wqkv), (wup_h, wup_pairs), (wdown_h, wdown), (wout_h, wout))
    ):
        loads.append(pltpu.make_async_copy(src, dst, local_sem.at[i]))
    loads[0].start()

    barrier = pltpu.get_barrier_semaphore()
    peers = [above, below, left, right, twin] + x_peer[1:] + zy_peer[2:]
    for peer in peers:
        pl.semaphore_signal(barrier, inc=1, device_id=peer, device_id_type=MESH)

    lane = lax.broadcasted_iota(jnp.int32, (1, INNER), 1) // 64
    same_head = (
        lax.broadcasted_iota(jnp.int32, (INNER, INNER), 0) // 64
        == lax.broadcasted_iota(jnp.int32, (INNER, INNER), 1) // 64
    )
    ones = jnp.where(same_head, 1.0, 0.0).astype(BF16)

    def head_sum(values):
        high = values.astype(BF16)
        low = (values - high.astype(F32)).astype(BF16)
        return nn(high, ones) + nn(low, ones)

    def head_rows(values):
        return [jnp.where(lane == h, values, jnp.zeros_like(values)) for h in range(4)]

    scale = jnp.zeros((1, INNER), F32)
    for h in range(4):
        scale = jnp.where(lane == h, head_scale[h], scale)

    toks = to_halves(tok[...].astype(F32))
    a = (toks * norm_scale(toks) * attn_gain[...]).astype(BF16)
    ain[...] = a
    fgrad[...] = to_halves(gout[...].astype(F32)).astype(BF16)
    loads[0].wait()
    for load in loads[1:]:
        load.start()
    key_raw = nn(a, wqkv[1])
    key_norm = lax.rsqrt(head_sum(key_raw * key_raw) + EPS)
    keys = (key_raw * key_norm).astype(BF16)
    win[0, 1, 1] = keys[:HALF]
    win[0, 2, 1] = keys[HALF:]
    raw[2] = key_raw
    raw[3] = key_norm
    pl.semaphore_wait(barrier, len(peers))

    def vertical(kv):
        return [
            links.start(win.at[kv, pl.ds(1, 2), 1], win.at[kv, pl.ds(1, 2), 0], below),
            links.start(win.at[kv, pl.ds(1, 2), 1], win.at[kv, pl.ds(1, 2), 2], above),
        ]

    def horizontal(kv, i):
        return [
            links.start(win.at[kv, 2, i], win.at[kv, 0, i], right),
            links.start(win.at[kv, 1, i], win.at[kv, 3, i], left),
        ]

    key_vert = vertical(0)
    key_side = horizontal(0, 1)
    values = nn(a, wqkv[2]).astype(BF16)
    win[1, 1, 1] = values[:HALF]
    win[1, 2, 1] = values[HALF:]
    value_vert = vertical(1)
    value_side = horizontal(1, 1)

    query_raw = nn(a, wqkv[0])
    query_norm = lax.rsqrt(head_sum(query_raw * query_raw) + EPS)
    raw[0] = query_raw
    raw[1] = query_norm
    queries = (query_raw * query_norm * scale).astype(BF16)
    for h, part in enumerate(head_rows(queries)):
        qmask[h * TOK : (h + 1) * TOK, :] = part

    def bias_rows(i, carry):
        t = lax.broadcasted_iota(jnp.int32, (32, KEYS), 0) + i * 32
        k = lax.broadcasted_iota(jnp.int32, (32, KEYS), 1)
        j = (
            jnp.where(k >= 192, 1, 0) + jnp.where(k >= 384, 1, 0) + jnp.where(k >= 576, 1, 0)
        )
        in_strip = k - 192 * j
        key_row = (in_strip >> 3) - 8
        key_col = (j - 1) * 8 + (k & 7)
        query_row = (t & 63) >> 3
        query_col = (t >> 6) * 8 + (t & 7)
        down, across_by = key_row - query_row, key_col - query_col
        at_row, at_col = row * 8 + key_row, col * 16 + key_col
        ok = (down >= -RADIUS) & (down <= RADIUS)
        ok = ok & (across_by >= -RADIUS) & (across_by <= RADIUS)
        ok = ok & (at_row >= 0) & (at_row < 8 * NROW) & (at_col >= 0) & (at_col < 16 * NCOL)
        bias[pl.ds(pl.multiple_of(i * 32, 32), 32), :] = jnp.where(ok, 0.0, -1e30)
        return carry

    lax.fori_loop(0, 4, bias_rows, 0)

    def part_rows(i, carry):
        rows = pl.ds(pl.multiple_of(i * 32, 32), 32)
        both = wup_pairs[rows]
        wup[rows, :HID] = both[:, 0, :]
        wup[rows, HID:] = both[:, 1, :]
        return carry

    loads[1].wait()
    lax.fori_loop(0, 8, part_rows, 0)
    for copy in key_vert:
        copy.wait_recv()
    key_side += horizontal(0, 0) + horizontal(0, 2)
    lax.fori_loop(8, 16, part_rows, 0)
    for copy in key_side:
        copy.wait_recv()

    key_window = win[0].reshape(KEYS, INNER)
    probs[...] = nt(qmask[...], key_window)
    for copy in value_vert:
        copy.wait_recv()
    value_side += horizontal(1, 0) + horizontal(1, 2)

    for i in range(16):
        rows = pl.ds(i * 32, 32)
        s = probs[rows, :] + bias[pl.ds((i % 4) * 32, 32), :]
        e = jnp.exp(s - jnp.max(s, axis=-1, keepdims=True))
        p = e * (1.0 / jnp.sum(e, axis=-1, keepdims=True))
        probs[rows, :] = p
        plow[rows, :] = p.astype(BF16)
    at = lax.broadcasted_iota(jnp.int32, (WIDTH, WIDTH), 0)
    of = lax.broadcasted_iota(jnp.int32, (WIDTH, WIDTH), 1)
    to = ((of >> 2) & 1) * 256 + (of >> 7) * 64 + ((of >> 3) & 7) * 8
    to = to + ((of >> 6) & 1) * 4 + (of & 3)
    order[...] = jnp.where(at == to, 1.0, 0.0).astype(BF16)
    left_t[0] = nt(order[...], fgrad[...]).astype(BF16)
    left_t[1] = nt(order[...], ain[...]).astype(BF16)

    loads[2].wait()
    loads[3].wait()
    ghid[...] = nt(fgrad[...], wdown[...])

    for copy in value_side:
        copy.wait_recv()
    value_window = win[1].reshape(KEYS, INNER)

    def fold_heads(stacked):
        total = jnp.where(lane == 0, stacked[:TOK], 0.0)
        for h in range(1, 4):
            total = total + jnp.where(lane == h, stacked[h * TOK : (h + 1) * TOK], 0.0)
        return total

    attended = fold_heads(nn(plow[...], value_window)).astype(BF16)
    att[...] = attended

    def exchange(slot, product):
        copies = []
        for half in range(2):
            sums[slot, half] = product(slice(half * INNER, (half + 1) * INNER)).astype(BF16)
            copies.append(links.start(sums.at[slot, half], sums_in.at[slot, half], twin))
        return copies

    def total_of(slot, copies):
        for copy in copies:
            copy.wait_recv()
        halves = [sums[slot, i].astype(F32) + sums_in[slot, i].astype(F32) for i in range(2)]
        return jnp.concatenate(halves, axis=1)

    attn_sum = exchange(0, lambda c: nn(attended, wout[:, c]))
    residual = to_halves(tok[...].astype(F32)) + total_of(0, attn_sum)
    resid[...] = residual
    m = (residual * norm_scale(residual) * mlp_gain[...]).astype(BF16)
    mlpin[...] = m

    for j in range(4):
        cols = slice(j * 256, (j + 1) * 256)
        cols_v = slice(HID + j * 256, HID + (j + 1) * 256)
        gate = nn(m, wup[:, cols])
        val = nn(m, wup[:, cols_v])
        cdf = 0.5 * (1.0 + erf(gate * 0.7071067811865476))
        density = jnp.exp(-0.5 * gate * gate) * 0.3989422804014327
        act = gate * cdf
        hidden[:, cols] = (act * val).astype(BF16)
        gh = ghid[:, cols]
        gmix[:, cols] = (gh * val * (cdf + gate * density)).astype(BF16)
        gmix[:, cols_v] = (gh * act).astype(BF16)
    mlp_back = exchange(1, lambda c: nt(gmix[...], wup[c, :]))

    down_p.fill(left_t.at[0], hidden[...])
    down_p.core()
    left_t[2] = nt(order[...], mlpin[...]).astype(BF16)
    up_p.fill(left_t.at[2], gmix[...])
    up_p.core()
    down_p.x1()

    grad_resid = to_halves(gout[...].astype(F32)) + norm_back(
        resid[...], mlp_gain[...], total_of(1, mlp_back)
    )
    gresid[...] = grad_resid
    grad_low = grad_resid.astype(BF16)
    grad_att = nt(grad_low, wout[...]).astype(BF16)
    for h, part in enumerate(head_rows(grad_att)):
        gmask[h * TOK : (h + 1) * TOK, :] = part

    def rims(kv, whole):
        whole = whole.reshape(4, 3, HALF, INNER)
        acc[kv] = whole[1:3]
        rim_out[kv, 0] = whole[0].astype(BF16)
        rim_out[kv, 1] = whole[3].astype(BF16)
        return [
            links.start(rim_out.at[kv, 0], rim_in.at[kv, 0], left),
            links.start(rim_out.at[kv, 1], rim_in.at[kv, 1], right),
        ]

    value_rims = rims(1, tn(plow[...], gmask[...]))
    up_p.x1()
    mlp_sum = exchange(2, lambda c: nn(hidden[...], wdown[:, c]))
    dprob[...] = nt(gmask[...], win[1].reshape(KEYS, INNER))

    for i in range(16):
        rows = pl.ds(i * 32, 32)
        p, g = probs[rows, :], dprob[rows, :]
        delta = jnp.sum(p * g, axis=-1, keepdims=True)
        dscore[rows, :] = (p * (g - delta)).astype(BF16)

    key_rims = rims(0, tn(dscore[...], qmask[...]))
    down_p.x2()

    def through_norm(which, incoming, factor):
        v, r = raw[2 * which], raw[2 * which + 1]
        along = head_sum(v * incoming)
        return factor * r * (incoming - r * r * v * along)

    grad_query = fold_heads(nn(dscore[...], win[0].reshape(KEYS, INNER)))
    gproj[:, :INNER] = through_norm(0, grad_query, scale).astype(BF16)
    left_t[3] = nt(order[...], gresid[...].astype(BF16)).astype(BF16)
    oq_p.fill(left_t.at[3], att[...])
    oq_p.fill(left_t.at[1], gproj[:, :INNER], INNER)
    oq_p.core()

    def turn(kv, copies):
        for copy in copies:
            copy.wait_recv()
        acc[kv, 1] = acc[kv, 1] + rim_in[kv, 0].astype(F32)
        acc[kv, 0] = acc[kv, 0] + rim_in[kv, 1].astype(F32)
        ver_out[kv, 0] = acc[kv, :, 0].astype(BF16)
        ver_out[kv, 1] = acc[kv, :, 2].astype(BF16)
        return [
            links.start(ver_out.at[kv, 0], ver_in.at[kv, 0], above),
            links.start(ver_out.at[kv, 1], ver_in.at[kv, 1], below),
        ]

    value_turn = turn(1, value_rims)
    key_turn = turn(0, key_rims)
    up_p.x2()
    down_p.z()
    out_o[...] = from_halves(resid[...] + total_of(2, mlp_sum)).astype(BF16)
    oq_p.x1()

    def owned(kv, copies):
        for copy in copies:
            copy.wait_recv()
        mine = acc[kv, :, 1] + ver_in[kv, 0].astype(F32) + ver_in[kv, 1].astype(F32)
        return mine.reshape(TOK, INNER)

    gproj[:, 2 * INNER :] = owned(1, value_turn).astype(BF16)
    kv_p.core(1, left_t.at[1], gproj[:, 2 * INNER :])
    gproj[:, INNER : 2 * INNER] = through_norm(1, owned(0, key_turn), 1.0).astype(BF16)
    kv_p.core(0, left_t.at[1], gproj[:, INNER : 2 * INNER])

    def in_part(c):
        part = nt(gproj[:, :INNER], wqkv[0, c, :])
        part = part + nt(gproj[:, INNER : 2 * INNER], wqkv[1, c, :])
        return part + nt(gproj[:, 2 * INNER :], wqkv[2, c, :])

    in_back = exchange(3, in_part)
    kv_p.x(1)
    up_p.z()
    kv_p.x(0)
    oq_p.x2()
    down_p.y()
    grad_in = gresid[...] + norm_back(
        to_halves(tok[...].astype(F32)), attn_gain[...], total_of(3, in_back)
    )
    gin_o[...] = from_halves(grad_in).astype(BF16)
    oq_p.z()
    kv_p.zy()
    up_p.y()
    oq_p.y()
    down_p.store()
    up_p.store()
    oq_p.store()
    kv_p.store()
    links.finish()


def laid_out(out, gin, gdown, gup, goq, gkv, out_o, gin_o, gqkv_o, gout_o, gup_o, gdown_o):
    out_o[...] = out[...]
    gin_o[...] = gin[...]
    gdown_o[...] = gdown[...]
    gout_o[...] = goq[:, :INNER]
    gqkv_o[0] = goq[:, INNER:]
    gqkv_o[1] = gkv[:, :INNER]
    gqkv_o[2] = gkv[:, INNER:]
    both = gup[...].astype(F32)
    for r in range(4):
        pair = jnp.concatenate([both[r : r + 1, :HID], both[r : r + 1, HID:]], axis=0)
        gup_o[r] = pair.astype(BF16)


def shards(tokens, grad_output, attn_gain, mlp_gain, w_qkv, w_out, w_up, w_down, head_scale):
    rows, cols, width = tokens.shape
    vmem = pl.BlockSpec(memory_space=pltpu.VMEM)
    anywhere = pl.BlockSpec(memory_space=pl.ANY)
    out_shape = [
        jax.ShapeDtypeStruct(tokens.shape, BF16),
        jax.ShapeDtypeStruct(tokens.shape, BF16),
    ] + [jax.ShapeDtypeStruct((4, n), BF16) for n in PIECES]
    scratch = []
    for n in PIECES[:3]:
        scratch += piece_scratch(n)
    scratch += last_scratch(PIECES[3])
    scratch += [
        pltpu.VMEM((3, WIDTH, INNER), BF16),
        pltpu.VMEM((INNER, WIDTH), BF16),
        pltpu.VMEM((WIDTH, 2 * HID), BF16),
        pltpu.VMEM((WIDTH, 2, HID), BF16),
        pltpu.VMEM((HID, WIDTH), BF16),
        pltpu.VMEM((2, 4, 3, HALF, INNER), BF16),
        pltpu.VMEM((4 * TOK, INNER), BF16),
        pltpu.VMEM((4 * TOK, INNER), BF16),
        pltpu.VMEM((TOK, KEYS), F32),
        pltpu.VMEM((4 * TOK, KEYS), F32),
        pltpu.VMEM((4 * TOK, KEYS), BF16),
        pltpu.VMEM((4 * TOK, KEYS), F32),
        pltpu.VMEM((4 * TOK, KEYS), BF16),
        pltpu.VMEM((4, TOK, INNER), F32),
        pltpu.VMEM((TOK, WIDTH), F32),
        pltpu.VMEM((TOK, WIDTH), F32),
        pltpu.VMEM((TOK, WIDTH), BF16),
        pltpu.VMEM((TOK, WIDTH), BF16),
        pltpu.VMEM((TOK, WIDTH), BF16),
        pltpu.VMEM((WIDTH, WIDTH), BF16),
        pltpu.VMEM((4, WIDTH, TOK), BF16),
        pltpu.VMEM((TOK, INNER), BF16),
        pltpu.VMEM((TOK, HID), F32),
        pltpu.VMEM((TOK, HID), BF16),
        pltpu.VMEM((TOK, 2 * HID), BF16),
        pltpu.VMEM((TOK, 3 * INNER), BF16),
        pltpu.VMEM((4, 2, TOK, INNER), BF16),
        pltpu.VMEM((4, 2, TOK, INNER), BF16),
        pltpu.VMEM((2, 2, 3, HALF, INNER), F32),
        pltpu.VMEM((2, 2, 3, HALF, INNER), BF16),
        pltpu.VMEM((2, 2, 3, HALF, INNER), BF16),
        pltpu.VMEM((2, 2, 2, HALF, INNER), BF16),
        pltpu.VMEM((2, 2, 2, HALF, INNER), BF16),
        pltpu.SemaphoreType.DMA((MESSAGES,)),
        pltpu.SemaphoreType.DMA((MESSAGES,)),
        pltpu.SemaphoreType.DMA((4,)),
    ]
    out, grad_input, gdown, gup, goq, gkv = pl.pallas_call(
        kernel,
        out_shape=out_shape,
        in_specs=[vmem] * 4
        + [pl.BlockSpec(memory_space=pltpu.SMEM)]
        + [anywhere] * 4,
        out_specs=[vmem] * 6,
        scratch_shapes=scratch,
        compiler_params=pltpu.CompilerParams(
            collective_id=0, has_side_effects=True, vmem_limit_bytes=58 * 1024 * 1024
        ),
    )(
        tokens,
        grad_output,
        attn_gain.reshape(1, width),
        mlp_gain.reshape(1, width),
        head_scale,
        jnp.transpose(w_qkv, (1, 0, 2)),
        w_out,
        w_up,
        w_down,
    )
    out, grad_input, grad_qkv, grad_out_t, grad_up, grad_down_t = pl.pallas_call(
        laid_out,
        out_shape=[
            jax.ShapeDtypeStruct(tokens.shape, BF16),
            jax.ShapeDtypeStruct(tokens.shape, BF16),
            jax.ShapeDtypeStruct((3, 4, INNER), BF16),
            jax.ShapeDtypeStruct((4, INNER), BF16),
            jax.ShapeDtypeStruct((4, 2, HID), BF16),
            jax.ShapeDtypeStruct((4, HID), BF16),
        ],
        in_specs=[vmem] * 6,
        out_specs=[vmem] * 6,
    )(out, grad_input, gdown, gup, goq, gkv)
    return out, grad_input, jnp.transpose(grad_qkv, (1, 0, 2)), grad_out_t, grad_up, grad_down_t


def solution(mesh):
    placed = (
        P("row", "col", None),
        P("row", "col", None),
        P(),
        P(),
        P(None, None, "ch"),
        P("ch", None),
        P(None, None, "ch"),
        P("ch", None),
        P("ch"),
    )
    return jax.shard_map(
        shards,
        mesh=mesh,
        in_specs=placed,
        out_specs=(
            P("row", "col", None),
            P("row", "col", None),
            P(("row", "col"), None, "ch"),
            P(("row", "col"), "ch"),
            P(("row", "col"), None, "ch"),
            P(("row", "col"), "ch"),
        ),
        check_vma=False,
    )
```
